256 devices in a mesh: dp: 64 (over y_hi, z, x), group: 4 (over y_lo, core).
Axes of the slice: x: 4, y: 4 (y_hi: 2, y_lo: 2; y = y_hi * 2 + y_lo), z: 8, core: 2. Of those that a mesh axis runs over, the one named last changes fastest.
Arguments:
- acts: bfloat16 [2, 16384, 256], P(None, 'dp'), may hold values from -16 to 16
- out_grads: bfloat16 [2, 16384, 16384], P(None, 'dp', 'group'), may hold values from -0.046875 to 0.046875
- master: float32 [2, 256, 16384], P(None, 'dp', 'group'), may hold values from -0.078125 to 0.078125
- m_codes: int32 [2, 256, 16384], P(None, 'dp', 'group'), may hold values from -127 to 127
- m_scale: float32 [2, 256, 8], P(None, 'dp', 'group'), may hold values from 0.1 to 1
- v_codes: int32 [2, 256, 16384], P(None, 'dp', 'group'), may hold values from 1 to 255
- v_scale: float32 [2, 256, 8], P(None, 'dp', 'group'), may hold values from 0.001 to 0.02
Outputs:
- new_master: float32 [2, 256, 16384], P(None, 'dp', 'group')
- m_state: float32 [2, 256, 16384], P(None, 'dp', 'group')
- m_absmax: float32 [2, 256, 8], P(None, 'dp', 'group')
- v_state: float32 [2, 256, 16384], P(None, 'dp', 'group')
- v_absmax: float32 [2, 256, 8], P(None, 'dp', 'group')
- rollout: bfloat16 [2, 256, 16384], P(None, None, 'dp')
The draws below stay inside these ranges and needn't reach their ends.
All inputs are finite; a program needn't handle non-finite values. Where the reference program divides by a largest or mean magnitude, that divisor is 1e-20 or more.
Results may differ from the reference program's by a relative error of at most 0.001.
Values may be sent and summed in bfloat16 or wider, within the bound.
No kernel may reach another device: no remote copies, remote signals or barrier semaphores. Data moves between devices by JAX's collectives and lax.ppermute only.
A program may use at most 64 MiB of HBM per device.

```python
import math
import jax
import jax.numpy as jnp
from jax import lax

FF = 16384
ROWS = 256
BLOCK = 2048
TOKENS = 16384
NBLK = 8


def touch_ends(entries, key, least, top_value):
    spot = [jax.random.randint(jax.random.fold_in(key, axis), (), 0, length) for axis, length in enumerate(entries.shape)]
    longest = entries.shape.index(max(entries.shape))
    next_to = spot[:longest] + [(spot[longest] + 1) % entries.shape[longest]] + spot[longest + 1:]
    return entries.at[tuple(spot)].set(least).at[tuple(next_to)].set(top_value)


def strengthened(array, key, source, target, shards_of, factor):
    def block_of(dim):
        return (jnp.arange(array.shape[dim]) // (array.shape[dim] // shards_of)).reshape((-1,) + (1,) * (array.ndim - 1 - dim))

    first = jax.random.permutation(key, shards_of)[block_of(target)]
    far = (block_of(target) + shards_of // 2) % shards_of
    return jnp.where((block_of(source) == first) | (block_of(source) == far), factor * array, array)


def steps_of(own_key, extent, shards, least, high):
    def one(dim, blocks):
        steps = jax.random.uniform(jax.random.fold_in(jax.random.fold_in(own_key, 6), dim), (blocks,), jnp.float32, least / len(shards), high / len(shards))
        return jnp.repeat(jnp.exp(steps), extent[dim] // blocks).reshape((-1,) + (1,) * (len(extent) - dim - 1))

    loudness = one(*shards[0])
    for cut in shards[1:]:
        loudness = loudness * one(*cut)
    return loudness


def normal_values(own_key, shape, width, bound, cuts=(), dtype=jnp.bfloat16):
    array = width * jax.random.normal(own_key, shape, jnp.float32)
    if cuts:
        array = array * steps_of(own_key, shape, cuts, -0.22, 0.18)
    return jnp.clip(array, -bound, bound).astype(dtype)


def bell_draw_with(stream_key, dims, scale, bound, split, heavy, dtype=jnp.bfloat16):
    drawn = scale * jax.random.normal(stream_key, dims, jnp.float32)
    if split:
        drawn = drawn * steps_of(stream_key, dims, split, -0.22, 0.18)
    return jnp.clip(strengthened(drawn, jax.random.fold_in(stream_key, 3), *heavy), -bound, bound).astype(dtype)


def setup_inputs(seed: int = 0) -> dict:
    seeds = jax.random.split(jax.random.key(seed), 8)
    acts = bell_draw_with(seeds[0], (2, TOKENS, ROWS), 1.0, 16.0, ((1, 64),), (1, 2, 64, 4.0))
    out_grads = normal_values(seeds[1], (2, TOKENS, FF), TOKENS ** -0.5, 0.046875, ((1, 64), (2, 4)))
    master = normal_values(seeds[2], (2, ROWS, FF), 0.005, 0.078125, ((1, 64), (2, 4)), jnp.float32)
    m_codes = touch_ends(jax.random.randint(seeds[3], (2, ROWS, FF), -127, 128), jax.random.fold_in(seeds[3], 1), -127, 127).astype(jnp.int32)
    m_scale = jnp.clip(jnp.exp(math.log(1.0) - 2.3025851 * jax.random.uniform(seeds[4], (2, ROWS, NBLK), jnp.float32) ** steps_of(seeds[4], (2, ROWS, NBLK), ((1, 64), (2, 4)), -0.2, 0.2)), 0.1, 1.0)
    v_codes = touch_ends(jax.random.randint(seeds[5], (2, ROWS, FF), 1, 256), jax.random.fold_in(seeds[5], 1), 1, 255).astype(jnp.int32)
    v_scale = jnp.clip(jnp.exp(math.log(0.02) - 2.9957322 * jax.random.uniform(seeds[6], (2, ROWS, NBLK), jnp.float32) ** steps_of(seeds[6], (2, ROWS, NBLK), ((1, 64), (2, 4)), -0.2, 0.2)), 0.001, 0.02)
    return dict(acts=acts, out_grads=out_grads, master=master, m_codes=m_codes, m_scale=m_scale, v_codes=v_codes, v_scale=v_scale)


beta_first = 0.9
beta_second = 0.999
first_bias = 1.0 - 0.9 ** 10
second_bias = 1.0 - 0.999 ** 10
learn_rate = 0.001
decay_rate = 0.1
adam_eps = 1e-08
scale_eps = 1e-06

def blocked(values):
    return values.reshape(values.shape[:-1] + (values.shape[-1] // BLOCK, BLOCK))

def adam_step(gradient, master, m_codes, m_scale, v_codes, v_scale):
    full_shape = gradient.shape
    m_old = blocked(m_codes.astype(jnp.float32)) * (m_scale[..., None] / 127.0)
    v_old = blocked(v_codes.astype(jnp.float32)) * (v_scale[..., None] / 255.0)
    grad_blocks = blocked(gradient)
    m_new = beta_first * m_old + (1.0 - beta_first) * grad_blocks
    v_new = beta_second * v_old + (1.0 - beta_second) * grad_blocks * grad_blocks
    update = m_new / first_bias / (jnp.sqrt(v_new / second_bias) + adam_eps)
    new_master = master - learn_rate * (update.reshape(full_shape) + decay_rate * master)
    m_absmax = lax.optimization_barrier(jnp.max(jnp.abs(m_new), axis=-1))
    m_state = (m_new / (m_absmax[..., None] + scale_eps)).reshape(full_shape)
    v_absmax = lax.optimization_barrier(jnp.max(v_new, axis=-1))
    v_state = (v_new / (v_absmax[..., None] + scale_eps)).reshape(full_shape)
    return (new_master, m_state, m_absmax, v_state, v_absmax)

def reference(acts, out_grads, master, m_codes, m_scale, v_codes, v_scale):

    def one_expert(operands):
        features, upstream = operands
        return jnp.dot(features.T, upstream, preferred_element_type=jnp.float32)
    gradient = lax.map(one_expert, (acts, out_grads))
    new_master, m_state, m_absmax, v_state, v_absmax = adam_step(gradient, master, m_codes, m_scale, v_codes, v_scale)
    rollout = new_master.astype(jnp.bfloat16)
    return (new_master, m_state, m_absmax, v_state, v_absmax, rollout)
```

```python
import functools

import jax
import jax.numpy as jnp
from jax import lax
from jax.experimental import pallas as pl
from jax.experimental.pallas import tpu as pltpu
from jax.sharding import PartitionSpec as P

BLOCK = 2048
LANES = 128
TOP = 32700.0
STEPS = 16.0

beta_first = 0.9
beta_second = 0.999
first_bias = 1.0 - 0.9**10
second_bias = 1.0 - 0.999**10
learn_rate = 0.001
decay_rate = 0.1
adam_eps = 1e-08
scale_eps = 1e-06

FIRST = 2560

PARAMS = pltpu.CompilerParams(vmem_limit_bytes=48 * 1024 * 1024)

Z_GROUPS = [[y * 32 + z * 4 + x for z in range(8)] for y in range(2) for x in range(4)]
YX_GROUPS = [[y * 32 + z * 4 + x for y in range(2) for x in range(4)] for z in range(8)]


def z_shift(k):
    return [
        (y * 32 + z * 4 + x, y * 32 + ((z + k) % 8) * 4 + x)
        for y in range(2)
        for z in range(8)
        for x in range(4)
    ]


def level_of(top):
    return jnp.ceil(STEPS * jnp.log2(jnp.maximum(top, 1e-30)))


def step_of(level):
    return jnp.exp2(level * (1.0 / STEPS)) * (1.0 / TOP)


def unit_of(level):
    return jnp.exp2(level * (-1.0 / STEPS)) * TOP


def coded(values, unit):
    return jnp.round(values * unit).astype(jnp.int32).astype(jnp.int16)


def decoded(codes):
    return codes.astype(jnp.int32).astype(jnp.float32)


def lane_max(top, values):
    for j in range(values.shape[1] // LANES):
        top = jnp.maximum(top, jnp.abs(values[:, j * LANES : (j + 1) * LANES]))
    return top


def pieces(width, size):
    return [(at, min(size, width - at)) for at in range(0, width, size)]


def partial_kernel(z_first, zs_ref, acts_ref, grads_ref, *rest):
    outs, sums = rest[:-1], rest[-1]
    width = grads_ref.shape[2]
    new = lax.broadcasted_iota(jnp.int32, (256, 256), 0)
    row = lax.broadcasted_iota(jnp.int32, (256, 256), 1)
    i = new & 3
    if z_first:
        x, y = (new >> 2) & 3, (new >> 4) & 1
        z = ((new >> 5) + zs_ref[0]) & 7
    else:
        z, x, y = (new >> 2) & 7, (new >> 5) & 3, new >> 7
    pick = jnp.where(row == y * 128 + z * 16 + x * 4 + i, 1.0, 0.0).astype(jnp.bfloat16)
    lhs = lax.dot_general(
        pick, acts_ref[0], (((1,), (1,)), ((), ())), preferred_element_type=jnp.float32
    ).astype(jnp.bfloat16)
    top = jnp.zeros((256, LANES), jnp.float32)
    for at, size in pieces(width, 512):
        part = jnp.dot(lhs, grads_ref[0, :, at : at + size], preferred_element_type=jnp.float32)
        sums[:, at : at + size] = part
        top = lane_max(top, part)
    level = level_of(jnp.max(top, axis=1, keepdims=True))
    unit = unit_of(level)
    note = jnp.broadcast_to(level, (256, LANES)).astype(jnp.int32).astype(jnp.int16)
    for b in range(8):
        rows = slice(b * 32, (b + 1) * 32)
        out = outs[b].at[0] if z_first else outs[0].at[b, 0]
        for at, size in pieces(width, 512):
            out[:, at : at + size] = coded(sums[rows, at : at + size], unit[rows])
        out[:, width:] = note[rows]


def partial_codes(acts, out_grads, zs, start, width, z_first):
    block = (2, 32, width + LANES)
    if z_first:
        out_shape = [jax.ShapeDtypeStruct(block, jnp.int16)] * 8
        out_specs = [pl.BlockSpec((1, 32, width + LANES), lambda e: (e, 0, 0))] * 8
    else:
        out_shape = [jax.ShapeDtypeStruct((8,) + block, jnp.int16)]
        out_specs = [pl.BlockSpec((8, 1, 32, width + LANES), lambda e: (0, e, 0, 0))]
    return pl.pallas_call(
        functools.partial(partial_kernel, z_first),
        grid=(2,),
        in_specs=[
            pl.BlockSpec(memory_space=pltpu.SMEM),
            pl.BlockSpec((1, 256, 256), lambda e: (e, 0, 0)),
            pl.BlockSpec((pl.Element(1), pl.Element(256), pl.Element(width)), lambda e: (e, 0, start)),
        ],
        out_shape=out_shape,
        out_specs=out_specs,
        scratch_shapes=[pltpu.VMEM((256, width), jnp.float32)],
        compiler_params=PARAMS,
        cost_estimate=pl.CostEstimate(
            flops=2 * 2 * 256 * 256 * width, bytes_accessed=2 * 256 * width * 4, transcendentals=0
        ),
    )(zs, acts, out_grads)


def regroup_kernel(*refs):
    *ins, out, sums = refs
    width = sums.shape[2]
    half = width // 2
    sources = [ins[0].at[s] for s in range(8)] if len(ins) == 1 else list(ins)
    for e in range(2):
        steps = [step_of(decoded(s[e, :, width:])[:, :1]) for s in sources]
        for at, size in pieces(width, 256):
            total = decoded(sources[0][e, :, at : at + size]) * steps[0]
            for s in range(1, 8):
                total = total + decoded(sources[s][e, :, at : at + size]) * steps[s]
            sums[e, :, at : at + size] = total
    upper = lax.broadcasted_iota(jnp.int32, (8, 1), 0) < 4
    for h in range(2):
        for b in range(0, 8, 2):
            tile = slice(b * 4, b * 4 + 8)
            first = sums[0, tile, h * half : (h + 1) * half]
            second = sums[1, tile, h * half : (h + 1) * half]
            even = jnp.where(upper, first, pltpu.roll(second, 4, 0))
            odd = jnp.where(upper, pltpu.roll(first, 4, 0), second)
            for k, values in ((b, even), (b + 1, odd)):
                top = lane_max(jnp.zeros((8, LANES), jnp.float32), values)
                level = level_of(jnp.max(top, axis=1, keepdims=True))
                note = jnp.broadcast_to(level, (8, LANES)).astype(jnp.int32).astype(jnp.int16)
                out[k, h * 8 : (h + 1) * 8, :half] = coded(values, unit_of(level))
                out[k, h * 8 : (h + 1) * 8, half:] = note


def regroup(received, width):
    return pl.pallas_call(
        regroup_kernel,
        out_shape=jax.ShapeDtypeStruct((8, 16, width // 2 + LANES), jnp.int16),
        scratch_shapes=[pltpu.VMEM((2, 32, width), jnp.float32)],
        compiler_params=PARAMS,
        cost_estimate=pl.CostEstimate(flops=8 * 64 * width * 4, bytes_accessed=8 * 64 * width * 2, transcendentals=0),
    )(*received)


def adam_kernel(a_ref, b_ref, master, m_codes, m_scale, v_codes, v_scale,
                new_master, m_state, m_absmax, v_state, v_absmax, rollout, grad):
    start = 0
    for ref in (a_ref, b_ref):
        half = ref.shape[2] - LANES
        total = None
        for s in range(8):
            term = decoded(ref[s, :, :half]) * step_of(decoded(ref[s, :, half:])[:, :1])
            total = term if total is None else total + term
        for h in range(2):
            grad[:, start : start + half] = total[h * 8 : (h + 1) * 8]
            start += half
    for e in range(2):
        for b in range(2):
            cols = slice(b * BLOCK, (b + 1) * BLOCK)
            g = grad[e * 4 : (e + 1) * 4, cols]
            m_old = m_codes[e, :, cols].astype(jnp.float32) * (m_scale[e, :, b : b + 1] / 127.0)
            v_old = v_codes[e, :, cols].astype(jnp.float32) * (v_scale[e, :, b : b + 1] / 255.0)
            m_new = beta_first * m_old + (1.0 - beta_first) * g
            v_new = beta_second * v_old + (1.0 - beta_second) * g * g
            update = m_new / first_bias / (jnp.sqrt(v_new / second_bias) + adam_eps)
            old = master[e, :, cols]
            new = old - learn_rate * (update + decay_rate * old)
            new_master[e, :, cols] = new
            m_top = jnp.max(jnp.abs(m_new), axis=1, keepdims=True)
            v_top = jnp.max(v_new, axis=1, keepdims=True)
            m_absmax[e, :, b : b + 1] = m_top
            v_absmax[e, :, b : b + 1] = v_top
            m_state[e, :, cols] = m_new / (m_top + scale_eps)
            v_state[e, :, cols] = v_new / (v_top + scale_eps)
            grad[e * 4 : (e + 1) * 4, cols] = new
    for k in range(16):
        for h in range(2):
            at = k * 256 + h * LANES
            rollout[k, h * 8 : (h + 1) * 8, :] = grad[:, at : at + LANES].astype(jnp.bfloat16)


def adam(a, b, master, m_codes, m_scale, v_codes, v_scale):
    big = jax.ShapeDtypeStruct((2, 4, 4096), jnp.float32)
    small = jax.ShapeDtypeStruct((2, 4, 2), jnp.float32)
    return pl.pallas_call(
        adam_kernel,
        out_shape=[big, big, small, big, small, jax.ShapeDtypeStruct((16, 16, LANES), jnp.bfloat16)],
        scratch_shapes=[pltpu.VMEM((8, 4096), jnp.float32)],
        compiler_params=PARAMS,
        cost_estimate=pl.CostEstimate(flops=2 * 4 * 4096 * 40, bytes_accessed=2 << 20, transcendentals=0),
    )(a, b, master, m_codes, m_scale, v_codes, v_scale)


def push_weights(weights):
    gathered = lax.all_gather(weights, "group", axis=0, tiled=True)
    swapped = lax.all_to_all(gathered, "dp", split_axis=0, concat_axis=0, tiled=True)
    spread = swapped.reshape(64, 2, 2, 4, LANES)
    return jnp.transpose(spread, (2, 0, 3, 1, 4)).reshape(2, 256, 256)


def on_device(acts, out_grads, master, m_codes, m_scale, v_codes, v_scale):
    width = out_grads.shape[2]
    me = lax.axis_index("dp")
    zs = ((me >> 2) & 7).reshape(1).astype(jnp.int32)
    [first] = partial_codes(acts, out_grads, zs, 0, FIRST, False)
    second = partial_codes(acts, out_grads, zs, FIRST, width - FIRST, True)
    second = [second[0]] + [lax.ppermute(second[k], "dp", z_shift(k)) for k in range(1, 8)]
    first = lax.all_to_all(first, "dp", 0, 0, axis_index_groups=YX_GROUPS, tiled=True)
    first = regroup([first], FIRST)
    second = regroup(second, width - FIRST)
    first = lax.all_to_all(first, "dp", 0, 0, axis_index_groups=Z_GROUPS, tiled=True)
    second = lax.all_to_all(second, "dp", 0, 0, axis_index_groups=YX_GROUPS, tiled=True)
    *state, weights = adam(first, second, master, m_codes, m_scale, v_codes, v_scale)
    return (*state, push_weights(weights))


def solution(mesh):
    split = P(None, "dp", "group")
    return jax.shard_map(
        on_device,
        mesh=mesh,
        in_specs=(P(None, "dp", None),) + (split,) * 6,
        out_specs=(split,) * 5 + (P(None, None, "dp"),),
        check_vma=False,
    )
```

```python
import functools

import jax
import jax.numpy as jnp
from jax import lax
from jax.experimental import pallas as pl
from jax.experimental.pallas import tpu as pltpu
from jax.sharding import PartitionSpec as P

BLOCK = 2048
LANES = 128
TOP = 32700.0
STEPS = 16.0

beta_first = 0.9
beta_second = 0.999
first_bias = 1.0 - 0.9**10
second_bias = 1.0 - 0.999**10
learn_rate = 0.001
decay_rate = 0.1
adam_eps = 1e-08
scale_eps = 1e-06

PARAMS = pltpu.CompilerParams(vmem_limit_bytes=56 * 1024 * 1024)

CHUNK = 2048
TILES = CHUNK // LANES

NEAR = [
    [y * 32 + (2 * zz + zl) * 4 + x for y in range(2) for zl in range(2) for x in range(4)]
    for zz in range(4)
]


def far_shift(k):
    return [
        (y * 32 + z * 4 + x, y * 32 + (z + 2 * k) % 8 * 4 + x)
        for y in range(2)
        for z in range(8)
        for x in range(4)
    ]


def swap_groups():
    pairs = [((a, g), (g, a)) for a in range(4) for g in range(a)]
    pairs += [((0, 0), (1, 1)), ((2, 2), (3, 3))]
    return [[(a * 16 + k) * 4 + g for a, g in pair for k in range(16)] for pair in pairs]


def level_of(top):
    return jnp.ceil(STEPS * jnp.log2(jnp.maximum(top, 1e-30)))


def step_of(level):
    return jnp.exp2(level * (1.0 / STEPS)) * (1.0 / TOP)


def unit_of(level):
    return jnp.exp2(level * (-1.0 / STEPS)) * TOP


def to_short(values):
    return values.astype(jnp.int32).astype(jnp.int16)


def coded(values, unit):
    return to_short(jnp.round(values * unit))


def decoded(codes):
    return codes.astype(jnp.int32).astype(jnp.float32)


def lane_max(top, values):
    for j in range(values.shape[1] // LANES):
        top = jnp.maximum(top, jnp.abs(values[:, j * LANES : (j + 1) * LANES]))
    return top


def lane_index(rows):
    return lax.broadcasted_iota(jnp.int32, (rows, LANES), 1)


def partial_kernel(zz_ref, acts_ref, grads_ref, out, grads, sums, codes, notes, sems_in, sems_out):
    chunks = grads.shape[0] // 2
    steps = 2 * chunks

    def load(s):
        source = grads_ref.at[s // chunks, :, pl.ds(s % chunks * CHUNK, CHUNK)]
        return pltpu.make_async_copy(source, grads.at[s], sems_in.at[s])

    def store(s):
        return pltpu.make_async_copy(codes.at[s], out.at[:, pl.ds(s * TILES, TILES)], sems_out.at[s])

    for s in range(steps):
        load(s).start()
    new = lax.broadcasted_iota(jnp.int32, (256, 256), 0)
    row = lax.broadcasted_iota(jnp.int32, (256, 256), 1)
    i, k, x, zl, y = new & 3, (new >> 2) & 3, (new >> 4) & 3, (new >> 6) & 1, new >> 7
    zz = (zz_ref[0] + k) & 3
    pick = jnp.where(row == y * 128 + zz * 32 + zl * 16 + x * 4 + i, 1.0, 0.0).astype(jnp.bfloat16)
    lane = lane_index(256)
    note = jnp.zeros((256, LANES), jnp.int32)
    for s in range(steps):
        if s % chunks == 0:
            lhs = lax.dot_general(
                pick, acts_ref[s // chunks], (((1,), (1,)), ((), ())), preferred_element_type=jnp.float32
            ).astype(jnp.bfloat16)
        load(s).wait()
        top = jnp.zeros((256, LANES), jnp.float32)
        for at in range(0, CHUNK, 512):
            part = jnp.dot(lhs, grads[s, :, at : at + 512], preferred_element_type=jnp.float32)
            sums[s % 2, :, at : at + 512] = part
            top = lane_max(top, part)
        level = level_of(jnp.max(top, axis=1, keepdims=True))
        unit = unit_of(level)
        note = jnp.where(lane == s, level.astype(jnp.int32), note)
        for b in range(16):
            rows = slice(b * 16, (b + 1) * 16)
            for t in range(TILES):
                codes[s, b, t] = coded(sums[s % 2, rows, t * LANES : (t + 1) * LANES], unit[rows])
        store(s).start()
    for b in range(16):
        notes[b, 0] = note[b * 16 : (b + 1) * 16].astype(jnp.int16)
    final = pltpu.make_async_copy(notes, out.at[:, pl.ds(steps * TILES, 1)], sems_out.at[steps])
    final.start()
    for s in range(steps):
        store(s).wait()
    final.wait()


def partial_codes(zz, acts, out_grads):
    steps = 2 * out_grads.shape[2] // CHUNK
    return pl.pallas_call(
        partial_kernel,
        in_specs=[
            pl.BlockSpec(memory_space=pltpu.SMEM),
            pl.BlockSpec(memory_space=pltpu.VMEM),
            pl.BlockSpec(memory_space=pl.ANY),
        ],
        out_shape=jax.ShapeDtypeStruct((16, steps * TILES + 1, 16, LANES), jnp.int16),
        out_specs=pl.BlockSpec(memory_space=pl.ANY),
        scratch_shapes=[
            pltpu.VMEM((steps, 256, CHUNK), jnp.bfloat16),
            pltpu.VMEM((2, 256, CHUNK), jnp.float32),
            pltpu.VMEM((steps, 16, TILES, 16, LANES), jnp.int16),
            pltpu.VMEM((16, 1, 16, LANES), jnp.int16),
            pltpu.SemaphoreType.DMA((steps,)),
            pltpu.SemaphoreType.DMA((steps + 1,)),
        ],
        compiler_params=PARAMS,
        cost_estimate=pl.CostEstimate(
            flops=4 * 256 * 256 * 4096, bytes_accessed=8 << 20, transcendentals=0
        ),
    )(zz, acts, out_grads)


def regroup_kernel(received, *rest):
    *outs, codes, notes, sums, sems = rest
    steps = codes.shape[0]
    chunks = steps // 2
    final = pltpu.make_async_copy(received.at[:, pl.ds(steps * TILES, 1)], notes, sems.at[steps])
    final.start()

    def load(s):
        return pltpu.make_async_copy(received.at[:, pl.ds(s * TILES, TILES)], codes.at[s], sems.at[s])

    for s in range(steps):
        load(s).start()
    final.wait()
    levels = [decoded(notes[n, 0]) for n in range(16)]
    for s in range(steps):
        scales = [step_of(level[:, s : s + 1]) for level in levels]
        load(s).wait()
        for t in range(TILES):
            total = decoded(codes[s, 0, t]) * scales[0]
            for n in range(1, 16):
                total = total + decoded(codes[s, n, t]) * scales[n]
            at = s % chunks * CHUNK + t * LANES
            sums[s // chunks, :, at : at + LANES] = total
    upper = lax.broadcasted_iota(jnp.int32, (8, 1), 0) < 4
    for pair in range(2):
        tile = slice(pair * 8, pair * 8 + 8)
        z = [[sums[e, tile, h * BLOCK : (h + 1) * BLOCK] for h in range(2)] for e in range(2)]
        even = [jnp.where(upper, z[0][h], pltpu.roll(z[1][h], 4, 0)) for h in range(2)]
        odd = [jnp.where(upper, pltpu.roll(z[0][h], 4, 0), z[1][h]) for h in range(2)]
        for out, halves in ((outs[pair * 2], even), (outs[pair * 2 + 1], odd)):
            values = jnp.concatenate(halves, axis=0)
            top = lane_max(jnp.zeros((16, LANES), jnp.float32), values)
            level = level_of(jnp.max(top, axis=1, keepdims=True))
            unit = unit_of(level)
            for t in range(16):
                out[t] = coded(values[:, t * LANES : (t + 1) * LANES], unit)
            out[16] = to_short(jnp.broadcast_to(level, (16, LANES)))


def regroup(received):
    steps = received.shape[1] // TILES
    return pl.pallas_call(
        regroup_kernel,
        in_specs=[pl.BlockSpec(memory_space=pl.ANY)],
        out_shape=[jax.ShapeDtypeStruct((17, 16, LANES), jnp.int16)] * 4,
        scratch_shapes=[
            pltpu.VMEM((steps, 16, TILES, 16, LANES), jnp.int16),
            pltpu.VMEM((16, 1, 16, LANES), jnp.int16),
            pltpu.VMEM((2, 16, 2 * BLOCK), jnp.float32),
            pltpu.SemaphoreType.DMA((steps + 1,)),
        ],
        compiler_params=PARAMS,
        cost_estimate=pl.CostEstimate(flops=4 << 20, bytes_accessed=4 << 20, transcendentals=0),
    )(received)


def adam_kernel(c0, c1, c2, c3, master, m_codes, m_scale, v_codes, v_scale,
                new_master, m_state, m_absmax, v_state, v_absmax, rollout, grad):
    codes = (c0, c1, c2, c3)
    steps = [step_of(decoded(c[16])[:, :1]) for c in codes]
    for t in range(16):
        total = decoded(c0[t]) * steps[0]
        for s in range(1, 4):
            total = total + decoded(codes[s][t]) * steps[s]
        for h in range(2):
            grad[:, h * BLOCK + t * LANES : h * BLOCK + (t + 1) * LANES] = total[h * 8 : (h + 1) * 8]
    for e in range(2):
        for b in range(2):
            cols = slice(b * BLOCK, (b + 1) * BLOCK)
            g = grad[e * 4 : (e + 1) * 4, cols]
            m_old = m_codes[e, :, cols].astype(jnp.float32) * (m_scale[e, :, b : b + 1] / 127.0)
            v_old = v_codes[e, :, cols].astype(jnp.float32) * (v_scale[e, :, b : b + 1] / 255.0)
            m_new = beta_first * m_old + (1.0 - beta_first) * g
            v_new = beta_second * v_old + (1.0 - beta_second) * g * g
            update = m_new / first_bias / (jnp.sqrt(v_new / second_bias) + adam_eps)
            old = master[e, :, cols]
            new = old - learn_rate * (update + decay_rate * old)
            new_master[e, :, cols] = new
            m_top = jnp.max(jnp.abs(m_new), axis=1, keepdims=True)
            v_top = jnp.max(v_new, axis=1, keepdims=True)
            m_absmax[e, :, b : b + 1] = m_top
            v_absmax[e, :, b : b + 1] = v_top
            m_state[e, :, cols] = m_new / (m_top + scale_eps)
            v_state[e, :, cols] = v_new / (v_top + scale_eps)
            grad[e * 4 : (e + 1) * 4, cols] = new
    for k in range(16):
        for h in range(2):
            at = k * 256 + h * LANES
            tile = grad[:, at : at + LANES].astype(jnp.bfloat16)
            for copy in range(2):
                rollout[copy * 16 + k, h * 8 : (h + 1) * 8, :] = tile


def adam(codes, master, m_codes, m_scale, v_codes, v_scale):
    big = jax.ShapeDtypeStruct((2, 4, 4096), jnp.float32)
    small = jax.ShapeDtypeStruct((2, 4, 2), jnp.float32)
    return pl.pallas_call(
        adam_kernel,
        out_shape=[big, big, small, big, small, jax.ShapeDtypeStruct((32, 16, LANES), jnp.bfloat16)],
        scratch_shapes=[pltpu.VMEM((8, 4096), jnp.float32)],
        compiler_params=PARAMS,
        cost_estimate=pl.CostEstimate(flops=2 * 4 * 4096 * 40, bytes_accessed=2 << 20, transcendentals=0),
    )(*codes, master, m_codes, m_scale, v_codes, v_scale)


def push_weights(weights):
    plane, group = lax.axis_index("dp") // 16, lax.axis_index("group")
    swapped = lax.all_to_all(
        weights, ("dp", "group"), 0, 0, axis_index_groups=swap_groups(), tiled=True
    )
    upper = jnp.where(plane == group, plane % 2 == 1, plane > group)
    slab = jnp.where(upper, swapped[16:], swapped[:16])
    gathered = lax.all_gather(slab, "group", axis=0, tiled=True)
    spread = gathered.reshape(64, 2, 2, 4, LANES)
    return jnp.transpose(spread, (2, 0, 3, 1, 4)).reshape(2, 256, 256)


def on_device(acts, out_grads, master, m_codes, m_scale, v_codes, v_scale):
    zz = ((lax.axis_index("dp") >> 3) & 3).reshape(1).astype(jnp.int32)
    codes = partial_codes(zz, acts, out_grads)
    codes = lax.all_to_all(codes, "dp", 0, 0, axis_index_groups=NEAR, tiled=True)
    codes = regroup(codes)
    codes = [codes[0]] + [lax.ppermute(codes[k], "dp", far_shift(k)) for k in range(1, 4)]
    *state, weights = adam(codes, master, m_codes, m_scale, v_codes, v_scale)
    return (*state, push_weights(weights))


def solution(mesh):
    split = P(None, "dp", "group")
    return jax.shard_map(
        on_device,
        mesh=mesh,
        in_specs=(P(None, "dp", None),) + (split,) * 6,
        out_specs=(split,) * 5 + (P(None, None, "dp"),),
        check_vma=False,
    )
```

```python
import functools

import jax
import jax.numpy as jnp
from jax import lax
from jax.experimental import pallas as pl
from jax.experimental.pallas import tpu as pltpu
from jax.sharding import PartitionSpec as P

BLOCK = 2048
LANES = 128
TOP = 32700.0
STEPS = 16.0

beta_first = 0.9
beta_second = 0.999
first_bias = 1.0 - 0.9**10
second_bias = 1.0 - 0.999**10
learn_rate = 0.001
decay_rate = 0.1
adam_eps = 1e-08
scale_eps = 1e-06

CHUNK = 1024
WIDTH = 4096
TILES = WIDTH // LANES

PARAMS = pltpu.CompilerParams(vmem_limit_bytes=20 * 1024 * 1024)
FIRST_PARAMS = pltpu.CompilerParams(vmem_limit_bytes=56 * 1024 * 1024)


def moved(step):
    def index(y, z, x):
        return y % 2 * 32 + z % 8 * 4 + x % 4

    return [(index(y, z, x), index(*step(y, z, x))) for y in range(2) for z in range(8) for x in range(4)]


UP = moved(lambda y, z, x: (y, z, x + 1))
DOWN = moved(lambda y, z, x: (y, z, x - 1))
PAIR = [moved(lambda y, z, x, e=e: (y, z + 1 if z % 2 == e else z - 1, x)) for e in range(2)]
ACROSS = moved(lambda y, z, x: (y + 1, z, x))


def z_shift(k):
    return moved(lambda y, z, x: (y, z + 2 * k, x))


def swap_groups():
    pairs = [((a, g), (g, a)) for a in range(4) for g in range(a)]
    pairs += [((0, 0), (1, 1)), ((2, 2), (3, 3))]
    return [[(a * 16 + k) * 4 + g for a, g in pair for k in range(16)] for pair in pairs]


def level_of(top):
    return jnp.ceil(STEPS * jnp.log2(jnp.maximum(top, 1e-30)))


def step_of(level):
    return jnp.exp2(level * (1.0 / STEPS)) * (1.0 / TOP)


def unit_of(level):
    return jnp.exp2(level * (-1.0 / STEPS)) * TOP


def to_short(values):
    return values.astype(jnp.int32).astype(jnp.int16)


def coded(values, unit):
    return to_short(jnp.round(values * unit))


def decoded(codes):
    return codes.astype(jnp.int32).astype(jnp.float32)


def lane_max(top, values):
    for j in range(values.shape[1] // LANES):
        top = jnp.maximum(top, jnp.abs(values[:, j * LANES : (j + 1) * LANES]))
    return top


def lane_index(rows):
    return lax.broadcasted_iota(jnp.int32, (rows, LANES), 1)


def picked(acts, expert, place, steps):
    y, z, x = place
    new = lax.broadcasted_iota(jnp.int32, (64, 256), 0)
    old = lax.broadcasted_iota(jnp.int32, (64, 256), 1)
    i, k, here_y, here_z = new & 3, (new >> 2) & 3, (new >> 4) & 1, new >> 5
    neighbour = jnp.where((z & 1) == expert, z + 1, z + 7)
    row_y = jnp.where(here_y == 1, y, 1 - y)
    row_z = (jnp.where(here_z == 1, z, neighbour) + 2 * k) & 7
    row = row_y * 128 + row_z * 16 + ((x + steps) & 3) * 4 + i
    pick = jnp.where(old == row, 1.0, 0.0).astype(jnp.bfloat16)
    return lax.dot_general(
        pick, acts, (((1,), (1,)), ((), ())), preferred_element_type=jnp.float32
    ).astype(jnp.bfloat16)


def add_up(steps, me, acts_ref, grads_ref, received, acts, grads, sums, sems):
    pieces = [(e, at) for e in range(2) for at in range(0, WIDTH, CHUNK)]

    def load(n):
        e, at = pieces[n]
        source = grads_ref.at[e, :, pl.ds(at, CHUNK)]
        return pltpu.make_async_copy(source, grads.at[e, :, pl.ds(at, CHUNK)], sems.at[n])

    load_acts = pltpu.make_async_copy(acts_ref, acts, sems.at[len(pieces)])
    load_acts.start()
    for n in range(len(pieces)):
        load(n).start()
    load_acts.wait()
    place = me >> 5, (me >> 2) & 7, me & 3
    lhs = [picked(acts[e], e, place, steps[e]) for e in range(2)]
    scales = []
    for e in range(2):
        notes = [decoded(r[4 * TILES]) for r in received[e]]
        scales.append([[step_of(note[:, g : g + 1]) for note in notes] for g in range(4)])
    tops = [[jnp.zeros((16, LANES), jnp.float32)] * 4 for _ in range(2)]
    for n, (e, first) in enumerate(pieces):
        load(n).wait()
        for at in range(first, first + CHUNK, 512):
            part = jnp.dot(lhs[e], grads[e, :, at : at + 512], preferred_element_type=jnp.float32)
            for g in range(4):
                for j in range(0, 512, LANES):
                    total = part[g * 16 : (g + 1) * 16, j : j + LANES]
                    for r, scale in zip(received[e], scales[e][g]):
                        total = total + decoded(r[g * TILES + (at + j) // LANES]) * scale
                    sums[e, g * 16 : (g + 1) * 16, at + j : at + j + LANES] = total
                    tops[e][g] = jnp.maximum(tops[e][g], jnp.abs(total))
    return tops


def codes_kernel(steps, me_ref, acts_ref, grads_ref, *rest):
    received, (out0, out1, acts, grads, sums, sems) = rest[:-6], rest[-6:]
    tops = add_up(steps, me_ref[0], acts_ref, grads_ref, [received[:1], received[1:]], acts, grads, sums, sems)
    for e, out in enumerate((out0, out1)):
        write_groups(out, [(sums.at[e], g, tops[e][g]) for g in range(4)])


def write_groups(out, groups):
    lane = lane_index(16)
    note = jnp.zeros((16, LANES), jnp.int32)
    for n, (sums, g, top) in enumerate(groups):
        level = level_of(jnp.max(top, axis=1, keepdims=True))
        unit = unit_of(level)
        note = jnp.where(lane == n, level.astype(jnp.int32), note)
        for t in range(TILES):
            out[n * TILES + t] = coded(sums[g * 16 : (g + 1) * 16, t * LANES : (t + 1) * LANES], unit)
    out[len(groups) * TILES] = note.astype(jnp.int16)


SPECS = [
    pl.BlockSpec(memory_space=pltpu.SMEM),
    pl.BlockSpec(memory_space=pl.ANY),
    pl.BlockSpec(memory_space=pl.ANY),
]


SCRATCH = [
    pltpu.VMEM((2, 256, 256), jnp.bfloat16),
    pltpu.VMEM((2, 256, WIDTH), jnp.bfloat16),
    pltpu.VMEM((2, 64, WIDTH), jnp.float32),
    pltpu.SemaphoreType.DMA((2 * WIDTH // CHUNK + 1,)),
]


COST = pl.CostEstimate(flops=4 * 64 * 256 * WIDTH, bytes_accessed=3 << 20, transcendentals=0)


def codes_for(steps, me, acts, out_grads, *received):
    return pl.pallas_call(
        functools.partial(codes_kernel, steps),
        in_specs=SPECS + [pl.BlockSpec(memory_space=pltpu.VMEM)] * len(received),
        out_shape=[jax.ShapeDtypeStruct((4 * TILES + 1, 16, LANES), jnp.int16)] * 2,
        scratch_shapes=SCRATCH,
        compiler_params=PARAMS if received else FIRST_PARAMS,
        cost_estimate=COST,
    )(me, acts, out_grads, *received)


def own_kernel(me_ref, acts_ref, grads_ref, a0, b0, a1, b1, out0, out1, kept, acts, grads, sums, sems):
    tops = add_up((0, 0), me_ref[0], acts_ref, grads_ref, [(a0, b0), (a1, b1)], acts, grads, sums, sems)
    for e, out in enumerate((out0, out1)):
        write_groups(out, [(sums.at[e], g, tops[e][g]) for g in range(2)])
        kept[e] = sums[e, 32:]


def own_codes(me, acts, out_grads, *received):
    codes = jax.ShapeDtypeStruct((2 * TILES + 1, 16, LANES), jnp.int16)
    return pl.pallas_call(
        own_kernel,
        in_specs=SPECS + [pl.BlockSpec(memory_space=pltpu.VMEM)] * 4,
        out_shape=[codes, codes, jax.ShapeDtypeStruct((2, 32, WIDTH), jnp.float32)],
        scratch_shapes=SCRATCH,
        compiler_params=PARAMS,
        cost_estimate=COST,
    )(me, acts, out_grads, *received)


def pair_kernel(kept, got0, got1, out, rest, sums):
    tops = []
    for e, got in enumerate((got0, got1)):
        note = decoded(got[2 * TILES])
        for g in range(2):
            scale = step_of(note[:, g : g + 1])
            top = jnp.zeros((16, LANES), jnp.float32)
            for t in range(TILES):
                cols = slice(t * LANES, (t + 1) * LANES)
                total = kept[e, g * 16 : (g + 1) * 16, cols] + decoded(got[g * TILES + t]) * scale
                if g == 0:
                    sums[e, :, cols] = total
                    top = jnp.maximum(top, jnp.abs(total))
                else:
                    rest[e, :, cols] = total
            if g == 0:
                tops.append(top)
    write_groups(out, [(sums.at[e], 0, tops[e]) for e in range(2)])


def pair_codes(kept, got0, got1):
    return pl.pallas_call(
        pair_kernel,
        out_shape=[
            jax.ShapeDtypeStruct((2 * TILES + 1, 16, LANES), jnp.int16),
            jax.ShapeDtypeStruct((2, 16, WIDTH), jnp.float32),
        ],
        scratch_shapes=[pltpu.VMEM((2, 16, WIDTH), jnp.float32)],
        compiler_params=PARAMS,
        cost_estimate=COST,
    )(kept, got0, got1)


def across_kernel(rest, got, *refs):
    *outs, sums = refs
    note = decoded(got[2 * TILES])
    for e in range(2):
        scale = step_of(note[:, e : e + 1])
        for t in range(TILES):
            cols = slice(t * LANES, (t + 1) * LANES)
            sums[e, :, cols] = rest[e, :, cols] + decoded(got[e * TILES + t]) * scale
    upper = lax.broadcasted_iota(jnp.int32, (8, 1), 0) < 4
    half = WIDTH // 2
    for pair in range(2):
        tile = slice(pair * 8, pair * 8 + 8)
        z = [[sums[e, tile, h * half : (h + 1) * half] for h in range(2)] for e in range(2)]
        even = [jnp.where(upper, z[0][h], pltpu.roll(z[1][h], 4, 0)) for h in range(2)]
        odd = [jnp.where(upper, pltpu.roll(z[0][h], 4, 0), z[1][h]) for h in range(2)]
        for out, halves in ((outs[pair * 2], even), (outs[pair * 2 + 1], odd)):
            values = jnp.concatenate(halves, axis=0)
            top = lane_max(jnp.zeros((16, LANES), jnp.float32), values)
            level = level_of(jnp.max(top, axis=1, keepdims=True))
            unit = unit_of(level)
            for t in range(TILES // 2):
                out[t] = coded(values[:, t * LANES : (t + 1) * LANES], unit)
            out[TILES // 2] = to_short(jnp.broadcast_to(level, (16, LANES)))


def across_codes(rest, got):
    return pl.pallas_call(
        across_kernel,
        out_shape=[jax.ShapeDtypeStruct((TILES // 2 + 1, 16, LANES), jnp.int16)] * 4,
        scratch_shapes=[pltpu.VMEM((2, 16, WIDTH), jnp.float32)],
        compiler_params=PARAMS,
        cost_estimate=COST,
    )(rest, got)


def adam_kernel(c0, c1, c2, c3, master, m_codes, m_scale, v_codes, v_scale,
                new_master, m_state, m_absmax, v_state, v_absmax, rollout, grad):
    codes = (c0, c1, c2, c3)
    tiles = TILES // 2
    steps = [step_of(decoded(c[tiles])[:, :1]) for c in codes]
    for t in range(tiles):
        total = decoded(c0[t]) * steps[0]
        for s in range(1, 4):
            total = total + decoded(codes[s][t]) * steps[s]
        for h in range(2):
            grad[:, (h * tiles + t) * LANES : (h * tiles + t + 1) * LANES] = total[h * 8 : (h + 1) * 8]
    diagonal = lax.broadcasted_iota(jnp.int32, (4, 4), 0) == lax.broadcasted_iota(jnp.int32, (4, 4), 1)

    def upright(row):
        return jnp.sum(jnp.where(diagonal, row, 0.0), axis=1, keepdims=True)

    def level_row(column):
        return jnp.sum(jnp.where(diagonal, column, 0.0), axis=0, keepdims=True)

    for e in range(2):
        for b in range(2):
            cols = slice(b * BLOCK, (b + 1) * BLOCK)
            g = grad[e * 4 : (e + 1) * 4, cols]
            m_old = m_codes[e, :, cols].astype(jnp.float32) * (upright(m_scale[e, b : b + 1, :]) / 127.0)
            v_old = v_codes[e, :, cols].astype(jnp.float32) * (upright(v_scale[e, b : b + 1, :]) / 255.0)
            m_new = beta_first * m_old + (1.0 - beta_first) * g
            v_new = beta_second * v_old + (1.0 - beta_second) * g * g
            update = m_new / first_bias / (jnp.sqrt(v_new / second_bias) + adam_eps)
            old = master[e, :, cols]
            new = old - learn_rate * (update + decay_rate * old)
            new_master[e, :, cols] = new
            m_top = jnp.max(jnp.abs(m_new), axis=1, keepdims=True)
            v_top = jnp.max(v_new, axis=1, keepdims=True)
            m_absmax[e, b : b + 1, :] = level_row(m_top)
            v_absmax[e, b : b + 1, :] = level_row(v_top)
            m_state[e, :, cols] = m_new / (m_top + scale_eps)
            v_state[e, :, cols] = v_new / (v_top + scale_eps)
            grad[e * 4 : (e + 1) * 4, cols] = new
    for k in range(16):
        for h in range(2):
            at = k * 256 + h * LANES
            tile = grad[:, at : at + LANES].astype(jnp.bfloat16)
            for copy in range(2):
                rollout[copy * 16 + k, h * 8 : (h + 1) * 8, :] = tile


def adam(codes, master, m_codes, m_scale, v_codes, v_scale):
    big = jax.ShapeDtypeStruct((2, 4, 4096), jnp.float32)
    small = jax.ShapeDtypeStruct((2, 2, 4), jnp.float32)
    new_master, m_state, m_absmax, v_state, v_absmax, weights = pl.pallas_call(
        adam_kernel,
        out_shape=[big, big, small, big, small, jax.ShapeDtypeStruct((32, 16, LANES), jnp.bfloat16)],
        scratch_shapes=[pltpu.VMEM((8, 4096), jnp.float32)],
        compiler_params=PARAMS,
        cost_estimate=pl.CostEstimate(flops=2 * 4 * 4096 * 40, bytes_accessed=2 << 20, transcendentals=0),
    )(*codes, master, m_codes, jnp.swapaxes(m_scale, 1, 2), v_codes, jnp.swapaxes(v_scale, 1, 2))
    return new_master, m_state, jnp.swapaxes(m_absmax, 1, 2), v_state, jnp.swapaxes(v_absmax, 1, 2), weights


def push_weights(weights):
    plane, group = lax.axis_index("dp") // 16, lax.axis_index("group")
    swapped = lax.all_to_all(
        weights, ("dp", "group"), 0, 0, axis_index_groups=swap_groups(), tiled=True
    )
    upper = jnp.where(plane == group, plane % 2 == 1, plane > group)
    slab = jnp.where(upper, swapped[16:], swapped[:16])
    slab = jnp.transpose(slab.reshape(16, 2, 2, 4, LANES), (2, 0, 3, 1, 4)).reshape(2, 64, 256)
    return lax.all_gather(slab, "group", axis=1, tiled=True)


def on_device(acts, out_grads, master, m_codes, m_scale, v_codes, v_scale):
    me = lax.axis_index("dp").reshape(1).astype(jnp.int32)

    far0, far1 = codes_for((2, 2), me, acts, out_grads)
    far0, far1 = lax.ppermute(far0, "dp", UP), lax.ppermute(far1, "dp", DOWN)
    down0, up1 = codes_for((3, 1), me, acts, out_grads)
    down0, up1 = lax.ppermute(down0, "dp", DOWN), lax.ppermute(up1, "dp", UP)
    up0, down1 = codes_for((1, 3), me, acts, out_grads, far0, far1)
    up0, down1 = lax.ppermute(up0, "dp", UP), lax.ppermute(down1, "dp", DOWN)
    near0, near1, kept = own_codes(me, acts, out_grads, down0, up0, up1, down1)
    near0, near1 = lax.ppermute(near0, "dp", PAIR[0]), lax.ppermute(near1, "dp", PAIR[1])
    across, rest = pair_codes(kept, near0, near1)
    codes = across_codes(rest, lax.ppermute(across, "dp", ACROSS))
    codes = [codes[0]] + [lax.ppermute(codes[k], "dp", z_shift(k)) for k in range(1, 4)]
    *state, weights = adam(codes, master, m_codes, m_scale, v_codes, v_scale)
    return (*state, push_weights(weights))


def solution(mesh):
    split = P(None, "dp", "group")
    return jax.shard_map(
        on_device,
        mesh=mesh,
        in_specs=(P(None, "dp", None),) + (split,) * 6,
        out_specs=(split,) * 5 + (P(None, None, "dp"),),
        check_vma=False,
    )
```

```python
import functools

import jax
import jax.numpy as jnp
from jax import lax
from jax.experimental import pallas as pl
from jax.experimental.pallas import tpu as pltpu
from jax.sharding import PartitionSpec as P

BLOCK = 2048
LANES = 128
TOP = 32700.0
STEPS = 16.0

beta_first = 0.9
beta_second = 0.999
first_bias = 1.0 - 0.9**10
second_bias = 1.0 - 0.999**10
learn_rate = 0.001
decay_rate = 0.1
adam_eps = 1e-08
scale_eps = 1e-06

PART_A = (0, 2560)
PART_B = (2560, 1536)
PIECE = 256

PARAMS = pltpu.CompilerParams(vmem_limit_bytes=20 * 1024 * 1024)
FIRST_PARAMS = pltpu.CompilerParams(vmem_limit_bytes=56 * 1024 * 1024)


def moved(step):
    def index(y, z, x):
        return y % 2 * 32 + z % 8 * 4 + x % 4

    return [(index(y, z, x), index(*step(y, z, x))) for y in range(2) for z in range(8) for x in range(4)]


UP = moved(lambda y, z, x: (y, z, x + 1))
DOWN = moved(lambda y, z, x: (y, z, x - 1))
TWO = moved(lambda y, z, x: (y, z, x + 2))
PAIR = [moved(lambda y, z, x, e=e: (y, z + 1 if z % 2 == e else z - 1, x)) for e in range(2)]
ACROSS = moved(lambda y, z, x: (y + 1, z, x))


def z_shift(k):
    return moved(lambda y, z, x: (y, z + 2 * k, x))


def swap_groups():
    pairs = [((a, g), (g, a)) for a in range(4) for g in range(a)]
    pairs += [((0, 0), (1, 1)), ((2, 2), (3, 3))]
    return [[(a * 16 + k) * 4 + g for a, g in pair for k in range(16)] for pair in pairs]


def level_of(top):
    return jnp.ceil(STEPS * jnp.log2(jnp.maximum(top, 1e-30)))


def step_of(level):
    return jnp.exp2(level * (1.0 / STEPS)) * (1.0 / TOP)


def unit_of(level):
    return jnp.exp2(level * (-1.0 / STEPS)) * TOP


def to_short(values):
    return values.astype(jnp.int32).astype(jnp.int16)


def coded(values, unit):
    return to_short(jnp.round(values * unit))


def decoded(codes):
    return codes.astype(jnp.int32).astype(jnp.float32)


def lane_max(top, values):
    for j in range(values.shape[1] // LANES):
        top = jnp.maximum(top, jnp.abs(values[:, j * LANES : (j + 1) * LANES]))
    return top


def lane_index(rows):
    return lax.broadcasted_iota(jnp.int32, (rows, LANES), 1)


def rows_a(steps):
    def rows(expert, place, new):
        y, z, x = place
        i, k, here_y, here_z = new & 3, (new >> 2) & 3, (new >> 4) & 1, new >> 5
        return old_row(expert, place, here_y, here_z, k, x + steps[expert], i)

    return rows


def rows_b(first_step, here_y):
    def rows(expert, place, new):
        i, k, here_z, step = new & 3, (new >> 2) & 3, (new >> 4) & 1, new >> 5
        return old_row(expert, place, here_y, here_z, k, place[2] + first_step + step, i)

    return rows


def old_row(expert, place, here_y, here_z, k, x, i):
    y, z, _ = place
    neighbour = jnp.where((z & 1) == expert, z + 1, z + 7)
    row_y = jnp.where(here_y == 1, y, 1 - y)
    row_z = (jnp.where(here_z == 1, z, neighbour) + 2 * k) & 7
    return row_y * 128 + row_z * 16 + (x & 3) * 4 + i


def picked(acts, expert, place, rows, count):
    new = lax.broadcasted_iota(jnp.int32, (count, 256), 0)
    old = lax.broadcasted_iota(jnp.int32, (count, 256), 1)
    pick = jnp.where(old == rows(expert, place, new), 1.0, 0.0).astype(jnp.bfloat16)
    return lax.dot_general(
        pick, acts, (((1,), (1,)), ((), ())), preferred_element_type=jnp.float32
    ).astype(jnp.bfloat16)


def add_up(part, rows, me_ref, acts_ref, grads_ref, received, acts, grads, sums, sems):
    start, width = part
    tiles, count = width // LANES, sums.shape[1] // 16
    pieces = [(e, at) for e in range(2) for at in range(0, width, width // 2)]

    def load(n):
        e, at = pieces[n]
        source = grads_ref.at[e, :, pl.ds(start + at, width // 2)]
        return pltpu.make_async_copy(source, grads.at[e, :, pl.ds(at, width // 2)], sems.at[n])

    load_acts = pltpu.make_async_copy(acts_ref, acts, sems.at[len(pieces)])
    load_acts.start()
    for n in range(len(pieces)):
        load(n).start()
    load_acts.wait()
    me = me_ref[0]
    place = me >> 5, (me >> 2) & 7, me & 3
    lhs = [picked(acts[e], e, place, rows, 16 * count) for e in range(2)]
    scales = []
    for e in range(2):
        notes = [decoded(r[r.shape[0] - 1]) for r, _ in received[e]]
        scales.append(
            [[step_of(note[:, at + g : at + g + 1]) for note, (_, at) in zip(notes, received[e])] for g in range(count)]
        )
    tops = [[jnp.zeros((16, LANES), jnp.float32)] * count for _ in range(2)]
    for n, (e, first) in enumerate(pieces):
        load(n).wait()
        for at in range(first, first + width // 2, PIECE):
            part_sums = jnp.dot(lhs[e], grads[e, :, at : at + PIECE], preferred_element_type=jnp.float32)
            for g in range(count):
                for j in range(0, PIECE, LANES):
                    total = part_sums[g * 16 : (g + 1) * 16, j : j + LANES]
                    for (r, group), scale in zip(received[e], scales[e][g]):
                        total = total + decoded(r[(group + g) * tiles + (at + j) // LANES]) * scale
                    sums[e, g * 16 : (g + 1) * 16, at + j : at + j + LANES] = total
                    tops[e][g] = jnp.maximum(tops[e][g], jnp.abs(total))
    return tops


def codes_kernel(steps, me_ref, acts_ref, grads_ref, *rest):
    got, (out0, out1, *work) = rest[:-6], rest[-6:]
    received = [[(r, 0) for r in got[e : e + 1]] for e in range(2)]
    tops = add_up(PART_A, rows_a(steps), me_ref, acts_ref, grads_ref, received, *work)
    sums = work[2]
    for e, out in enumerate((out0, out1)):
        write_groups(out, [(sums.at[e], g, tops[e][g]) for g in range(4)])


def write_groups(out, groups):
    tiles = (out.shape[0] - 1) // len(groups)
    lane = lane_index(16)
    note = jnp.zeros((16, LANES), jnp.int32)
    for n, (sums, g, top) in enumerate(groups):
        level = level_of(jnp.max(top, axis=1, keepdims=True))
        unit = unit_of(level)
        note = jnp.where(lane == n, level.astype(jnp.int32), note)
        for t in range(tiles):
            out[n * tiles + t] = coded(sums[g * 16 : (g + 1) * 16, t * LANES : (t + 1) * LANES], unit)
    out[len(groups) * tiles] = note.astype(jnp.int16)


SPECS = [
    pl.BlockSpec(memory_space=pltpu.SMEM),
    pl.BlockSpec(memory_space=pl.ANY),
    pl.BlockSpec(memory_space=pl.ANY),
]


VMEM = pl.BlockSpec(memory_space=pltpu.VMEM)


def scratch(part, rows):
    width = part[1]
    return [
        pltpu.VMEM((2, 256, 256), jnp.bfloat16),
        pltpu.VMEM((2, 256, width), jnp.bfloat16),
        pltpu.VMEM((2, rows, width), jnp.float32),
        pltpu.SemaphoreType.DMA((5,)),
    ]


def codes_of(groups, part):
    return jax.ShapeDtypeStruct((groups * part[1] // LANES + 1, 16, LANES), jnp.int16)


def sums_of(rows, part):
    return jax.ShapeDtypeStruct((2, rows, part[1]), jnp.float32)


COST = pl.CostEstimate(flops=4 * 64 * 256 * 4096, bytes_accessed=6 << 20, transcendentals=0)


def call(kernel, outs, work, ins, params=PARAMS, inputs=3):
    return pl.pallas_call(
        kernel,
        in_specs=SPECS[:inputs] + [VMEM] * (len(ins) - inputs),
        out_shape=outs,
        scratch_shapes=work,
        compiler_params=params,
        cost_estimate=COST,
    )(*ins)


def codes_for(steps, *ins):
    return call(functools.partial(codes_kernel, steps), [codes_of(4, PART_A)] * 2, scratch(PART_A, 64), ins)


def own_kernel(me_ref, acts_ref, grads_ref, a0, b0, a1, b1, out0, out1, kept, *work):
    received = [[(a0, 0), (b0, 0)], [(a1, 0), (b1, 0)]]
    tops = add_up(PART_A, rows_a((0, 0)), me_ref, acts_ref, grads_ref, received, *work)
    sums = work[2]
    for e, out in enumerate((out0, out1)):
        write_groups(out, [(sums.at[e], g, tops[e][g]) for g in range(2)])
        kept[e] = sums[e, 32:]


def own_codes(*ins):
    return call(own_kernel, [codes_of(2, PART_A)] * 2 + [sums_of(32, PART_A)], scratch(PART_A, 64), ins)


def pair_kernel(kept, got0, got1, out, rest, sums):
    tiles = PART_A[1] // LANES
    tops = []
    for e, got in enumerate((got0, got1)):
        note = decoded(got[2 * tiles])
        for g in range(2):
            scale = step_of(note[:, g : g + 1])
            top = jnp.zeros((16, LANES), jnp.float32)
            for t in range(tiles):
                cols = slice(t * LANES, (t + 1) * LANES)
                total = kept[e, g * 16 : (g + 1) * 16, cols] + decoded(got[g * tiles + t]) * scale
                if g == 0:
                    sums[e, :, cols] = total
                    top = jnp.maximum(top, jnp.abs(total))
                else:
                    rest[e, :, cols] = total
            if g == 0:
                tops.append(top)
    write_groups(out, [(sums.at[e], 0, tops[e]) for e in range(2)])


def pair_codes(*ins):
    outs = [codes_of(2, PART_A), sums_of(16, PART_A)]
    return call(pair_kernel, outs, [pltpu.VMEM((2, 16, PART_A[1]), jnp.float32)], ins, inputs=0)


def across_first_kernel(me_ref, acts_ref, grads_ref, out, *work):
    tops = add_up(PART_B, rows_b(0, 0), me_ref, acts_ref, grads_ref, [[], []], *work)
    write_groups(out, [(work[2].at[e], g, tops[e][g]) for e in range(2) for g in range(8)])


def across_first(*ins):
    return call(across_first_kernel, codes_of(16, PART_B), scratch(PART_B, 128), ins, FIRST_PARAMS)


def along_x_kernel(me_ref, acts_ref, grads_ref, got, out1, out2, out3, *work):
    received = [[(got, e * 8 + 2)] for e in range(2)]
    tops = add_up(PART_B, rows_b(1, 1), me_ref, acts_ref, grads_ref, received, *work)
    for k, out in enumerate((out1, out2, out3)):
        write_groups(out, [(work[2].at[e], g, tops[e][g]) for e in range(2) for g in (2 * k, 2 * k + 1)])


def along_x(*ins):
    return call(along_x_kernel, [codes_of(4, PART_B)] * 3, scratch(PART_B, 96), ins)


def own_b_kernel(me_ref, acts_ref, grads_ref, got, r1, r2, r3, out0, out1, kept, *work):
    received = [[(got, e * 8)] + [(r, e * 2) for r in (r1, r2, r3)] for e in range(2)]
    tops = add_up(PART_B, rows_b(0, 1), me_ref, acts_ref, grads_ref, received, *work)
    sums = work[2]
    for e, out in enumerate((out0, out1)):
        write_groups(out, [(sums.at[e], 0, tops[e][0])])
        kept[e] = sums[e, 16:]


def own_b_codes(*ins):
    return call(own_b_kernel, [codes_of(1, PART_B)] * 2 + [sums_of(16, PART_B)], scratch(PART_B, 32), ins)


def join_kernel(rest, got, kept, near0, near1, *refs):
    *outs, sums = refs
    tiles = PART_A[1] // LANES
    note = decoded(got[2 * tiles])
    for e in range(2):
        scale = step_of(note[:, e : e + 1])
        for t in range(tiles):
            cols = slice(t * LANES, (t + 1) * LANES)
            sums[e, :, cols] = rest[e, :, cols] + decoded(got[e * tiles + t]) * scale
        near = (near0, near1)[e]
        scale = step_of(decoded(near[near.shape[0] - 1])[:, :1])
        for t in range(PART_B[1] // LANES):
            at = PART_B[0] + t * LANES
            sums[e, :, at : at + LANES] = kept[e, :, t * LANES : (t + 1) * LANES] + decoded(near[t]) * scale
    upper = lax.broadcasted_iota(jnp.int32, (8, 1), 0) < 4
    for pair in range(2):
        tile = slice(pair * 8, pair * 8 + 8)
        z = [[sums[e, tile, h * BLOCK : (h + 1) * BLOCK] for h in range(2)] for e in range(2)]
        even = [jnp.where(upper, z[0][h], pltpu.roll(z[1][h], 4, 0)) for h in range(2)]
        odd = [jnp.where(upper, pltpu.roll(z[0][h], 4, 0), z[1][h]) for h in range(2)]
        for out, halves in ((outs[pair * 2], even), (outs[pair * 2 + 1], odd)):
            values = jnp.concatenate(halves, axis=0)
            top = lane_max(jnp.zeros((16, LANES), jnp.float32), values)
            level = level_of(jnp.max(top, axis=1, keepdims=True))
            unit = unit_of(level)
            for t in range(16):
                out[t] = coded(values[:, t * LANES : (t + 1) * LANES], unit)
            out[16] = to_short(jnp.broadcast_to(level, (16, LANES)))


def join(*ins):
    outs = [jax.ShapeDtypeStruct((17, 16, LANES), jnp.int16)] * 4
    return call(join_kernel, outs, [pltpu.VMEM((2, 16, 2 * BLOCK), jnp.float32)], ins, inputs=0)


def adam_kernel(c0, c1, c2, c3, master, m_codes, m_scale, v_codes, v_scale,
                new_master, m_state, m_absmax, v_state, v_absmax, rollout, grad):
    codes = (c0, c1, c2, c3)
    tiles = BLOCK // LANES
    steps = [step_of(decoded(c[tiles])[:, :1]) for c in codes]
    for t in range(tiles):
        total = decoded(c0[t]) * steps[0]
        for s in range(1, 4):
            total = total + decoded(codes[s][t]) * steps[s]
        for h in range(2):
            grad[:, (h * tiles + t) * LANES : (h * tiles + t + 1) * LANES] = total[h * 8 : (h + 1) * 8]
    diagonal = lax.broadcasted_iota(jnp.int32, (4, 4), 0) == lax.broadcasted_iota(jnp.int32, (4, 4), 1)

    def upright(row):
        return jnp.sum(jnp.where(diagonal, row, 0.0), axis=1, keepdims=True)

    def level_row(column):
        return jnp.sum(jnp.where(diagonal, column, 0.0), axis=0, keepdims=True)

    for e in range(2):
        for b in range(2):
            cols = slice(b * BLOCK, (b + 1) * BLOCK)
            g = grad[e * 4 : (e + 1) * 4, cols]
            m_old = m_codes[e, :, cols].astype(jnp.float32) * (upright(m_scale[e, b : b + 1, :]) / 127.0)
            v_old = v_codes[e, :, cols].astype(jnp.float32) * (upright(v_scale[e, b : b + 1, :]) / 255.0)
            m_new = beta_first * m_old + (1.0 - beta_first) * g
            v_new = beta_second * v_old + (1.0 - beta_second) * g * g
            update = m_new / first_bias / (jnp.sqrt(v_new / second_bias) + adam_eps)
            old = master[e, :, cols]
            new = old - learn_rate * (update + decay_rate * old)
            new_master[e, :, cols] = new
            m_top = jnp.max(jnp.abs(m_new), axis=1, keepdims=True)
            v_top = jnp.max(v_new, axis=1, keepdims=True)
            m_absmax[e, b : b + 1, :] = level_row(m_top)
            v_absmax[e, b : b + 1, :] = level_row(v_top)
            m_state[e, :, cols] = m_new / (m_top + scale_eps)
            v_state[e, :, cols] = v_new / (v_top + scale_eps)
            grad[e * 4 : (e + 1) * 4, cols] = new
    for k in range(16):
        for h in range(2):
            at = k * 256 + h * LANES
            tile = grad[:, at : at + LANES].astype(jnp.bfloat16)
            for copy in range(2):
                rollout[copy * 16 + k, h * 8 : (h + 1) * 8, :] = tile


def adam(codes, master, m_codes, m_scale, v_codes, v_scale):
    big = jax.ShapeDtypeStruct((2, 4, 4096), jnp.float32)
    small = jax.ShapeDtypeStruct((2, 2, 4), jnp.float32)
    new_master, m_state, m_absmax, v_state, v_absmax, weights = pl.pallas_call(
        adam_kernel,
        out_shape=[big, big, small, big, small, jax.ShapeDtypeStruct((32, 16, LANES), jnp.bfloat16)],
        scratch_shapes=[pltpu.VMEM((8, 4096), jnp.float32)],
        compiler_params=PARAMS,
        cost_estimate=pl.CostEstimate(flops=2 * 4 * 4096 * 40, bytes_accessed=2 << 20, transcendentals=0),
    )(*codes, master, m_codes, jnp.swapaxes(m_scale, 1, 2), v_codes, jnp.swapaxes(v_scale, 1, 2))
    return new_master, m_state, jnp.swapaxes(m_absmax, 1, 2), v_state, jnp.swapaxes(v_absmax, 1, 2), weights


def push_weights(weights):
    plane, group = lax.axis_index("dp") // 16, lax.axis_index("group")
    swapped = lax.all_to_all(
        weights, ("dp", "group"), 0, 0, axis_index_groups=swap_groups(), tiled=True
    )
    upper = jnp.where(plane == group, plane % 2 == 1, plane > group)
    slab = jnp.where(upper, swapped[16:], swapped[:16])
    slab = jnp.transpose(slab.reshape(16, 2, 2, 4, LANES), (2, 0, 3, 1, 4)).reshape(2, 64, 256)
    return lax.all_gather(slab, "group", axis=1, tiled=True)


def on_device(acts, out_grads, master, m_codes, m_scale, v_codes, v_scale):
    me = lax.axis_index("dp").reshape(1).astype(jnp.int32)

    inputs = (me, acts, out_grads)

    def send(codes, pairs):
        return lax.ppermute(codes, "dp", pairs)

    far0, far1 = codes_for((2, 2), *inputs)
    far0, far1 = send(far0, UP), send(far1, DOWN)
    crossed = send(across_first(*inputs), ACROSS)
    down0, up1 = codes_for((3, 1), *inputs)
    down0, up1 = send(down0, DOWN), send(up1, UP)
    up0, down1 = codes_for((1, 3), *inputs, far0, far1)
    up0, down1 = send(up0, UP), send(down1, DOWN)
    steps = along_x(*inputs, crossed)
    acts, _ = lax.optimization_barrier((acts, steps[0]))
    inputs = (me, acts, out_grads)
    steps = [send(steps[0], UP), send(steps[1], TWO), send(steps[2], DOWN)]
    near0, near1, kept = own_codes(*inputs, down0, up0, up1, down1)
    near0, near1 = send(near0, PAIR[0]), send(near1, PAIR[1])
    across, rest = pair_codes(kept, near0, near1)
    across = send(across, ACROSS)
    near0, near1, kept = own_b_codes(*inputs, crossed, *steps)
    near0, near1 = send(near0, PAIR[0]), send(near1, PAIR[1])
    codes = join(rest, across, kept, near0, near1)
    codes = [codes[0]] + [send(codes[k], z_shift(k)) for k in range(1, 4)]
    *state, weights = adam(codes, master, m_codes, m_scale, v_codes, v_scale)
    return (*state, push_weights(weights))


def solution(mesh):
    split = P(None, "dp", "group")
    return jax.shard_map(
        on_device,
        mesh=mesh,
        in_specs=(P(None, "dp", None),) + (split,) * 6,
        out_specs=(split,) * 5 + (P(None, None, "dp"),),
        check_vma=False,
    )
```

```python
import functools

import jax
import jax.numpy as jnp
from jax import lax
from jax.experimental import pallas as pl
from jax.experimental.pallas import tpu as pltpu
from jax.sharding import PartitionSpec as P

BLOCK = 2048
LANES = 128
TOP = 32700.0
STEPS = 16.0

beta_first = 0.9
beta_second = 0.999
first_bias = 1.0 - 0.9**10
second_bias = 1.0 - 0.999**10
learn_rate = 0.001
decay_rate = 0.1
adam_eps = 1e-08
scale_eps = 1e-06

PART_A = (0, 2560)
PART_B = (2560, 1536)
PIECE = 256

PARAMS = pltpu.CompilerParams(vmem_limit_bytes=20 * 1024 * 1024)
FIRST_PARAMS = pltpu.CompilerParams(vmem_limit_bytes=56 * 1024 * 1024)


def moved(step):
    def index(y, z, x):
        return y % 2 * 32 + z % 8 * 4 + x % 4

    return [(index(y, z, x), index(*step(y, z, x))) for y in range(2) for z in range(8) for x in range(4)]


UP = moved(lambda y, z, x: (y, z, x + 1))
DOWN = moved(lambda y, z, x: (y, z, x - 1))
TWO = moved(lambda y, z, x: (y, z, x + 2))
PAIR = [moved(lambda y, z, x, e=e: (y, z + 1 if z % 2 == e else z - 1, x)) for e in range(2)]
ACROSS = moved(lambda y, z, x: (y + 1, z, x))


def z_shift(k):
    return moved(lambda y, z, x: (y, z + 2 * k, x))


def swap_groups():
    pairs = [((a, g), (g, a)) for a in range(4) for g in range(a)]
    pairs += [((0, 0), (1, 1)), ((2, 2), (3, 3))]
    return [[(a * 16 + k) * 4 + g for a, g in pair for k in range(16)] for pair in pairs]


def level_of(top):
    return jnp.ceil(STEPS * jnp.log2(jnp.maximum(top, 1e-30)))


def step_of(level):
    return jnp.exp2(level * (1.0 / STEPS)) * (1.0 / TOP)


def unit_of(level):
    return jnp.exp2(level * (-1.0 / STEPS)) * TOP


def to_short(values):
    return values.astype(jnp.int32).astype(jnp.int16)


def coded(values, unit):
    return to_short(jnp.round(values * unit))


def decoded(codes):
    return codes.astype(jnp.int32).astype(jnp.float32)


def lane_max(top, values):
    for j in range(values.shape[1] // LANES):
        top = jnp.maximum(top, jnp.abs(values[:, j * LANES : (j + 1) * LANES]))
    return top


def lane_index(rows):
    return lax.broadcasted_iota(jnp.int32, (rows, LANES), 1)


def rows_a(steps):
    def rows(expert, place, new):
        y, z, x = place
        i, k, here_y, here_z = new & 3, (new >> 2) & 3, (new >> 4) & 1, new >> 5
        return old_row(expert, place, here_y, here_z, k, x + steps[expert], i)

    return rows


def rows_b(first_step, here_y, here_z=None):
    def rows(expert, place, new):
        i, k, step = new & 3, (new >> 2) & 3, new >> 4
        if here_z is None:
            return old_row(expert, place, here_y, step >> 2, k, place[2] + (step & 3), i)
        return old_row(expert, place, here_y, here_z, k, place[2] + first_step + step, i)

    return rows


def old_row(expert, place, here_y, here_z, k, x, i):
    y, z, _ = place
    neighbour = jnp.where((z & 1) == expert, z + 1, z + 7)
    row_y = jnp.where(here_y == 1, y, 1 - y)
    row_z = (jnp.where(here_z == 1, z, neighbour) + 2 * k) & 7
    return row_y * 128 + row_z * 16 + (x & 3) * 4 + i


def picked(acts, expert, place, rows, count):
    new = lax.broadcasted_iota(jnp.int32, (count, 256), 0)
    old = lax.broadcasted_iota(jnp.int32, (count, 256), 1)
    pick = jnp.where(old == rows(expert, place, new), 1.0, 0.0).astype(jnp.bfloat16)
    return lax.dot_general(
        pick, acts, (((1,), (1,)), ((), ())), preferred_element_type=jnp.float32
    ).astype(jnp.bfloat16)


def add_up(part, rows, me_ref, acts_ref, grads_ref, received, acts, grads, sums, sems):
    start, width = part
    tiles, count = width // LANES, sums.shape[1] // 16
    pieces = [(e, at) for e in range(2) for at in range(0, width, width // 2)]

    def load(n):
        e, at = pieces[n]
        source = grads_ref.at[e, :, pl.ds(start + at, width // 2)]
        return pltpu.make_async_copy(source, grads.at[e, :, pl.ds(at, width // 2)], sems.at[n])

    load_acts = pltpu.make_async_copy(acts_ref, acts, sems.at[len(pieces)])
    load_acts.start()
    for n in range(len(pieces)):
        load(n).start()
    load_acts.wait()
    me = me_ref[0]
    place = me >> 5, (me >> 2) & 7, me & 3
    lhs = [picked(acts[e], e, place, rows, 16 * count) for e in range(2)]
    scales = []
    for e in range(2):
        notes = [decoded(r[r.shape[0] - 1]) for r, _ in received[e]]
        scales.append(
            [[step_of(note[:, at + g : at + g + 1]) for note, (_, at) in zip(notes, received[e])] for g in range(count)]
        )
    tops = [[jnp.zeros((16, LANES), jnp.float32)] * count for _ in range(2)]
    for n, (e, first) in enumerate(pieces):
        load(n).wait()
        for at in range(first, first + width // 2, PIECE):
            part_sums = jnp.dot(lhs[e], grads[e, :, at : at + PIECE], preferred_element_type=jnp.float32)
            for g in range(count):
                for j in range(0, PIECE, LANES):
                    total = part_sums[g * 16 : (g + 1) * 16, j : j + LANES]
                    for (r, group), scale in zip(received[e], scales[e][g]):
                        total = total + decoded(r[(group + g) * tiles + (at + j) // LANES]) * scale
                    sums[e, g * 16 : (g + 1) * 16, at + j : at + j + LANES] = total
                    tops[e][g] = jnp.maximum(tops[e][g], jnp.abs(total))
    return tops


def codes_kernel(steps, me_ref, acts_ref, grads_ref, *rest):
    got, (out0, out1, *work) = rest[:-6], rest[-6:]
    received = [[(r, 0) for r in got[e : e + 1]] for e in range(2)]
    tops = add_up(PART_A, rows_a(steps), me_ref, acts_ref, grads_ref, received, *work)
    sums = work[2]
    for e, out in enumerate((out0, out1)):
        write_groups(out, [(sums.at[e], g, tops[e][g]) for g in range(4)])


def write_groups(out, groups):
    tiles = (out.shape[0] - 1) // len(groups)
    lane = lane_index(16)
    note = jnp.zeros((16, LANES), jnp.int32)
    for n, (sums, g, top) in enumerate(groups):
        level = level_of(jnp.max(top, axis=1, keepdims=True))
        unit = unit_of(level)
        note = jnp.where(lane == n, level.astype(jnp.int32), note)
        for t in range(tiles):
            out[n * tiles + t] = coded(sums[g * 16 : (g + 1) * 16, t * LANES : (t + 1) * LANES], unit)
    out[len(groups) * tiles] = note.astype(jnp.int16)


SPECS = [
    pl.BlockSpec(memory_space=pltpu.SMEM),
    pl.BlockSpec(memory_space=pl.ANY),
    pl.BlockSpec(memory_space=pl.ANY),
]


VMEM = pl.BlockSpec(memory_space=pltpu.VMEM)


def scratch(part, rows):
    width = part[1]
    return [
        pltpu.VMEM((2, 256, 256), jnp.bfloat16),
        pltpu.VMEM((2, 256, width), jnp.bfloat16),
        pltpu.VMEM((2, rows, width), jnp.float32),
        pltpu.SemaphoreType.DMA((5,)),
    ]


def codes_of(groups, part):
    return jax.ShapeDtypeStruct((groups * part[1] // LANES + 1, 16, LANES), jnp.int16)


def sums_of(rows, part):
    return jax.ShapeDtypeStruct((2, rows, part[1]), jnp.float32)


COST = pl.CostEstimate(flops=4 * 64 * 256 * 4096, bytes_accessed=6 << 20, transcendentals=0)


def call(kernel, outs, work, ins, params=PARAMS, inputs=3):
    return pl.pallas_call(
        kernel,
        in_specs=SPECS[:inputs] + [VMEM] * (len(ins) - inputs),
        out_shape=outs,
        scratch_shapes=work,
        compiler_params=params,
        cost_estimate=COST,
    )(*ins)


def codes_for(steps, *ins):
    return call(functools.partial(codes_kernel, steps), [codes_of(4, PART_A)] * 2, scratch(PART_A, 64), ins)


def own_kernel(me_ref, acts_ref, grads_ref, a0, b0, a1, b1, out0, out1, kept, *work):
    received = [[(a0, 0), (b0, 0)], [(a1, 0), (b1, 0)]]
    tops = add_up(PART_A, rows_a((0, 0)), me_ref, acts_ref, grads_ref, received, *work)
    sums = work[2]
    for e, out in enumerate((out0, out1)):
        write_groups(out, [(sums.at[e], g, tops[e][g]) for g in range(2)])
        kept[e] = sums[e, 32:]


def own_codes(*ins):
    return call(own_kernel, [codes_of(2, PART_A)] * 2 + [sums_of(32, PART_A)], scratch(PART_A, 64), ins)


def pair_kernel(kept, got0, got1, out, rest, sums):
    tiles = PART_A[1] // LANES
    tops = []
    for e, got in enumerate((got0, got1)):
        note = decoded(got[2 * tiles])
        for g in range(2):
            scale = step_of(note[:, g : g + 1])
            top = jnp.zeros((16, LANES), jnp.float32)
            for t in range(tiles):
                cols = slice(t * LANES, (t + 1) * LANES)
                total = kept[e, g * 16 : (g + 1) * 16, cols] + decoded(got[g * tiles + t]) * scale
                if g == 0:
                    sums[e, :, cols] = total
                    top = jnp.maximum(top, jnp.abs(total))
                else:
                    rest[e, :, cols] = total
            if g == 0:
                tops.append(top)
    write_groups(out, [(sums.at[e], 0, tops[e]) for e in range(2)])


def pair_codes(*ins):
    outs = [codes_of(2, PART_A), sums_of(16, PART_A)]
    return call(pair_kernel, outs, [pltpu.VMEM((2, 16, PART_A[1]), jnp.float32)], ins, inputs=0)


def across_first_kernel(me_ref, acts_ref, grads_ref, out, *work):
    tops = add_up(PART_B, rows_b(0, 0), me_ref, acts_ref, grads_ref, [[], []], *work)
    write_groups(out, [(work[2].at[e], g, tops[e][g]) for e in range(2) for g in range(8)])


def across_first(*ins):
    return call(across_first_kernel, codes_of(16, PART_B), scratch(PART_B, 128), ins, FIRST_PARAMS)


def near_kernel(me_ref, acts_ref, grads_ref, got, out0, out1, *work):
    received = [[(got, e * 8)] for e in range(2)]
    tops = add_up(PART_B, rows_b(0, 1, 0), me_ref, acts_ref, grads_ref, received, *work)
    for e, out in enumerate((out0, out1)):
        write_groups(out, [(work[2].at[e], g, tops[e][g]) for g in range(4)])


def near_codes(*ins):
    return call(near_kernel, [codes_of(4, PART_B)] * 2, scratch(PART_B, 64), ins)


def along_x_kernel(me_ref, acts_ref, grads_ref, got, near0, near1, out1, out2, out3, *work):
    received = [[(got, e * 8 + 5), ((near0, near1)[e], 1)] for e in range(2)]
    tops = add_up(PART_B, rows_b(1, 1, 1), me_ref, acts_ref, grads_ref, received, *work)
    for k, out in enumerate((out1, out2, out3)):
        write_groups(out, [(work[2].at[e], k, tops[e][k]) for e in range(2)])


def along_x(*ins):
    return call(along_x_kernel, [codes_of(2, PART_B)] * 3, scratch(PART_B, 48), ins)


def own_b_kernel(me_ref, acts_ref, grads_ref, got, near0, near1, r1, r2, r3, out, *work):
    received = [[(got, e * 8 + 4), ((near0, near1)[e], 0)] + [(r, e) for r in (r1, r2, r3)] for e in range(2)]
    add_up(PART_B, rows_b(0, 1, 1), me_ref, acts_ref, grads_ref, received, *work)
    out[...] = work[2][...]


def own_b(*ins):
    return call(own_b_kernel, sums_of(16, PART_B), scratch(PART_B, 16), ins)


def join_kernel(rest, got, own, *refs):
    *outs, sums = refs
    tiles = PART_A[1] // LANES
    note = decoded(got[2 * tiles])
    for e in range(2):
        scale = step_of(note[:, e : e + 1])
        for t in range(tiles):
            cols = slice(t * LANES, (t + 1) * LANES)
            sums[e, :, cols] = rest[e, :, cols] + decoded(got[e * tiles + t]) * scale
        sums[e, :, PART_B[0] :] = own[e]
    upper = lax.broadcasted_iota(jnp.int32, (8, 1), 0) < 4
    for pair in range(2):
        tile = slice(pair * 8, pair * 8 + 8)
        z = [[sums[e, tile, h * BLOCK : (h + 1) * BLOCK] for h in range(2)] for e in range(2)]
        even = [jnp.where(upper, z[0][h], pltpu.roll(z[1][h], 4, 0)) for h in range(2)]
        odd = [jnp.where(upper, pltpu.roll(z[0][h], 4, 0), z[1][h]) for h in range(2)]
        for out, halves in ((outs[pair * 2], even), (outs[pair * 2 + 1], odd)):
            values = jnp.concatenate(halves, axis=0)
            top = lane_max(jnp.zeros((16, LANES), jnp.float32), values)
            level = level_of(jnp.max(top, axis=1, keepdims=True))
            unit = unit_of(level)
            for t in range(16):
                out[t] = coded(values[:, t * LANES : (t + 1) * LANES], unit)
            out[16] = to_short(jnp.broadcast_to(level, (16, LANES)))


def join(*ins):
    outs = [jax.ShapeDtypeStruct((17, 16, LANES), jnp.int16)] * 4
    return call(join_kernel, outs, [pltpu.VMEM((2, 16, 2 * BLOCK), jnp.float32)], ins, inputs=0)


def adam_kernel(c0, c1, c2, c3, master, m_codes, m_scale, v_codes, v_scale,
                new_master, m_state, m_absmax, v_state, v_absmax, rollout, grad):
    codes = (c0, c1, c2, c3)
    tiles = BLOCK // LANES
    steps = [step_of(decoded(c[tiles])[:, :1]) for c in codes]
    for t in range(tiles):
        total = decoded(c0[t]) * steps[0]
        for s in range(1, 4):
            total = total + decoded(codes[s][t]) * steps[s]
        for h in range(2):
            grad[:, (h * tiles + t) * LANES : (h * tiles + t + 1) * LANES] = total[h * 8 : (h + 1) * 8]
    diagonal = lax.broadcasted_iota(jnp.int32, (4, 4), 0) == lax.broadcasted_iota(jnp.int32, (4, 4), 1)

    def upright(row):
        return jnp.sum(jnp.where(diagonal, row, 0.0), axis=1, keepdims=True)

    def level_row(column):
        return jnp.sum(jnp.where(diagonal, column, 0.0), axis=0, keepdims=True)

    for e in range(2):
        for b in range(2):
            cols = slice(b * BLOCK, (b + 1) * BLOCK)
            g = grad[e * 4 : (e + 1) * 4, cols]
            m_old = m_codes[e, :, cols].astype(jnp.float32) * (upright(m_scale[e, b : b + 1, :]) / 127.0)
            v_old = v_codes[e, :, cols].astype(jnp.float32) * (upright(v_scale[e, b : b + 1, :]) / 255.0)
            m_new = beta_first * m_old + (1.0 - beta_first) * g
            v_new = beta_second * v_old + (1.0 - beta_second) * g * g
            update = m_new / first_bias / (jnp.sqrt(v_new / second_bias) + adam_eps)
            old = master[e, :, cols]
            new = old - learn_rate * (update + decay_rate * old)
            new_master[e, :, cols] = new
            m_top = jnp.max(jnp.abs(m_new), axis=1, keepdims=True)
            v_top = jnp.max(v_new, axis=1, keepdims=True)
            m_absmax[e, b : b + 1, :] = level_row(m_top)
            v_absmax[e, b : b + 1, :] = level_row(v_top)
            m_state[e, :, cols] = m_new / (m_top + scale_eps)
            v_state[e, :, cols] = v_new / (v_top + scale_eps)
            grad[e * 4 : (e + 1) * 4, cols] = new
    for k in range(16):
        for h in range(2):
            at = k * 256 + h * LANES
            tile = grad[:, at : at + LANES].astype(jnp.bfloat16)
            for copy in range(2):
                rollout[copy * 16 + k, h * 8 : (h + 1) * 8, :] = tile


def adam(codes, master, m_codes, m_scale, v_codes, v_scale):
    big = jax.ShapeDtypeStruct((2, 4, 4096), jnp.float32)
    small = jax.ShapeDtypeStruct((2, 2, 4), jnp.float32)
    new_master, m_state, m_absmax, v_state, v_absmax, weights = pl.pallas_call(
        adam_kernel,
        out_shape=[big, big, small, big, small, jax.ShapeDtypeStruct((32, 16, LANES), jnp.bfloat16)],
        scratch_shapes=[pltpu.VMEM((8, 4096), jnp.float32)],
        compiler_params=PARAMS,
        cost_estimate=pl.CostEstimate(flops=2 * 4 * 4096 * 40, bytes_accessed=2 << 20, transcendentals=0),
    )(*codes, master, m_codes, jnp.swapaxes(m_scale, 1, 2), v_codes, jnp.swapaxes(v_scale, 1, 2))
    return new_master, m_state, jnp.swapaxes(m_absmax, 1, 2), v_state, jnp.swapaxes(v_absmax, 1, 2), weights


def push_weights(weights):
    plane, group = lax.axis_index("dp") // 16, lax.axis_index("group")
    swapped = lax.all_to_all(
        weights, ("dp", "group"), 0, 0, axis_index_groups=swap_groups(), tiled=True
    )
    upper = jnp.where(plane == group, plane % 2 == 1, plane > group)
    slab = jnp.where(upper, swapped[16:], swapped[:16])
    slab = jnp.transpose(slab.reshape(16, 2, 2, 4, LANES), (2, 0, 3, 1, 4)).reshape(2, 64, 256)
    return lax.all_gather(slab, "group", axis=1, tiled=True)


def on_device(acts, out_grads, master, m_codes, m_scale, v_codes, v_scale):
    me = lax.axis_index("dp").reshape(1).astype(jnp.int32)

    inputs = (me, acts, out_grads)

    def send(codes, pairs):
        return lax.ppermute(codes, "dp", pairs)

    far0, far1 = codes_for((2, 2), *inputs)
    far0, far1 = send(far0, UP), send(far1, DOWN)
    crossed = send(across_first(*inputs), ACROSS)
    down0, up1 = codes_for((3, 1), *inputs)
    down0, up1 = send(down0, DOWN), send(up1, UP)
    up0, down1 = codes_for((1, 3), *inputs, far0, far1)
    up0, down1 = send(up0, UP), send(down1, DOWN)
    there0, there1 = near_codes(*inputs, crossed)
    acts, _ = lax.optimization_barrier((acts, there0))
    there0, there1 = send(there0, PAIR[0]), send(there1, PAIR[1])
    inputs = (me, acts, out_grads)
    near0, near1, kept = own_codes(*inputs, down0, up0, up1, down1)
    near0, near1 = send(near0, PAIR[0]), send(near1, PAIR[1])
    steps = along_x(*inputs, crossed, there0, there1)
    kept, _ = lax.optimization_barrier((kept, steps[0]))
    steps = [send(steps[0], UP), send(steps[1], TWO), send(steps[2], DOWN)]
    across, rest = pair_codes(kept, near0, near1)
    across = send(across, ACROSS)
    own = own_b(*inputs, crossed, there0, there1, *steps)
    codes = join(rest, across, own)
    codes = [codes[0]] + [send(codes[k], z_shift(k)) for k in range(1, 4)]
    *state, weights = adam(codes, master, m_codes, m_scale, v_codes, v_scale)
    return (*state, push_weights(weights))


def solution(mesh):
    split = P(None, "dp", "group")
    return jax.shard_map(
        on_device,
        mesh=mesh,
        in_specs=(P(None, "dp", None),) + (split,) * 6,
        out_specs=(split,) * 5 + (P(None, None, "dp"),),
        check_vma=False,
    )
```

```python
import functools

import jax
import jax.numpy as jnp
from jax import lax
from jax.experimental import pallas as pl
from jax.experimental.pallas import tpu as pltpu
from jax.sharding import PartitionSpec as P

BLOCK = 2048
LANES = 128
TOP = 32700.0
STEPS = 16.0

beta_first = 0.9
beta_second = 0.999
first_bias = 1.0 - 0.9**10
second_bias = 1.0 - 0.999**10
learn_rate = 0.001
decay_rate = 0.1
adam_eps = 1e-08
scale_eps = 1e-06

PART_A = (0, 2560)
PART_B = (2560, 1536)
PIECE = 256

PARAMS = pltpu.CompilerParams(vmem_limit_bytes=20 * 1024 * 1024)
FIRST_PARAMS = pltpu.CompilerParams(vmem_limit_bytes=56 * 1024 * 1024)


def moved(step):
    def index(y, z, x):
        return y % 2 * 32 + z % 8 * 4 + x % 4

    return [(index(y, z, x), index(*step(y, z, x))) for y in range(2) for z in range(8) for x in range(4)]


UP = moved(lambda y, z, x: (y, z, x + 1))
DOWN = moved(lambda y, z, x: (y, z, x - 1))
TWO = moved(lambda y, z, x: (y, z, x + 2))
PAIR = [moved(lambda y, z, x, e=e: (y, z + 1 if z % 2 == e else z - 1, x)) for e in range(2)]
ACROSS = moved(lambda y, z, x: (y + 1, z, x))


def z_shift(k):
    return moved(lambda y, z, x: (y, z + 2 * k, x))


def swap_groups():
    pairs = [((a, g), (g, a)) for a in range(4) for g in range(a)]
    pairs += [((0, 0), (1, 1)), ((2, 2), (3, 3))]
    return [[(a * 16 + k) * 4 + g for a, g in pair for k in range(16)] for pair in pairs]


def level_of(top):
    return jnp.ceil(STEPS * jnp.log2(jnp.maximum(top, 1e-30)))


def step_of(level):
    return jnp.exp2(level * (1.0 / STEPS)) * (1.0 / TOP)


def unit_of(level):
    return jnp.exp2(level * (-1.0 / STEPS)) * TOP


def to_short(values):
    return values.astype(jnp.int32).astype(jnp.int16)


def coded(values, unit):
    return to_short(jnp.round(values * unit))


def decoded(codes):
    return codes.astype(jnp.int32).astype(jnp.float32)


def lane_max(top, values):
    for j in range(values.shape[1] // LANES):
        top = jnp.maximum(top, jnp.abs(values[:, j * LANES : (j + 1) * LANES]))
    return top


def lane_index(rows):
    return lax.broadcasted_iota(jnp.int32, (rows, LANES), 1)


def rows_a(steps):
    def rows(expert, place, new):
        y, z, x = place
        i, k, here_y, here_z = new & 3, (new >> 2) & 3, (new >> 4) & 1, new >> 5
        return old_row(expert, place, here_y, here_z, k, x + steps[expert], i)

    return rows


def rows_b(first_step, here_y, here_z=None):
    def rows(expert, place, new):
        i, k, step = new & 3, (new >> 2) & 3, new >> 4
        if here_z is None:
            return old_row(expert, place, here_y, step >> 2, k, place[2] + (step & 3), i)
        return old_row(expert, place, here_y, here_z, k, place[2] + first_step + step, i)

    return rows


def old_row(expert, place, here_y, here_z, k, x, i):
    y, z, _ = place
    neighbour = jnp.where((z & 1) == expert, z + 1, z + 7)
    row_y = jnp.where(here_y == 1, y, 1 - y)
    row_z = (jnp.where(here_z == 1, z, neighbour) + 2 * k) & 7
    return row_y * 128 + row_z * 16 + (x & 3) * 4 + i


def picked(acts, expert, place, rows, count):
    new = lax.broadcasted_iota(jnp.int32, (count, 256), 0)
    old = lax.broadcasted_iota(jnp.int32, (count, 256), 1)
    pick = jnp.where(old == rows(expert, place, new), 1.0, 0.0).astype(jnp.bfloat16)
    return lax.dot_general(
        pick, acts, (((1,), (1,)), ((), ())), preferred_element_type=jnp.float32
    ).astype(jnp.bfloat16)


def add_up(part, rows, me_ref, acts_ref, grads_ref, received, acts, grads, sums, sems):
    start, width = part
    tiles, count = width // LANES, sums.shape[1] // 16
    pieces = [(e, at) for e in range(2) for at in range(0, width, width // 2)]

    def load(n):
        e, at = pieces[n]
        source = grads_ref.at[e, :, pl.ds(start + at, width // 2)]
        return pltpu.make_async_copy(source, grads.at[e, :, pl.ds(at, width // 2)], sems.at[n])

    load_acts = pltpu.make_async_copy(acts_ref, acts, sems.at[len(pieces)])
    load_acts.start()
    for n in range(len(pieces)):
        load(n).start()
    load_acts.wait()
    me = me_ref[0]
    place = me >> 5, (me >> 2) & 7, me & 3
    lhs = [picked(acts[e], e, place, rows, 16 * count) for e in range(2)]
    scales = []
    for e in range(2):
        notes = [decoded(r[r.shape[0] - 1]) for r, _ in received[e]]
        scales.append(
            [[step_of(note[:, at + g : at + g + 1]) for note, (_, at) in zip(notes, received[e])] for g in range(count)]
        )
    tops = [[jnp.zeros((16, LANES), jnp.float32)] * count for _ in range(2)]
    for n, (e, first) in enumerate(pieces):
        load(n).wait()
        for at in range(first, first + width // 2, PIECE):
            part_sums = jnp.dot(lhs[e], grads[e, :, at : at + PIECE], preferred_element_type=jnp.float32)
            for g in range(count):
                for j in range(0, PIECE, LANES):
                    total = part_sums[g * 16 : (g + 1) * 16, j : j + LANES]
                    for (r, group), scale in zip(received[e], scales[e][g]):
                        total = total + decoded(r[(group + g) * tiles + (at + j) // LANES]) * scale
                    sums[e, g * 16 : (g + 1) * 16, at + j : at + j + LANES] = total
                    tops[e][g] = jnp.maximum(tops[e][g], jnp.abs(total))
    return tops


def codes_kernel(steps, me_ref, acts_ref, grads_ref, *rest):
    got, (out0, out1, *work) = rest[:-6], rest[-6:]
    received = [[(r, 0) for r in got[e : e + 1]] for e in range(2)]
    tops = add_up(PART_A, rows_a(steps), me_ref, acts_ref, grads_ref, received, *work)
    sums = work[2]
    for e, out in enumerate((out0, out1)):
        write_groups(out, [(sums.at[e], g, tops[e][g]) for g in range(4)])


def write_groups(out, groups):
    tiles = (out.shape[0] - 1) // len(groups)
    lane = lane_index(16)
    note = jnp.zeros((16, LANES), jnp.int32)
    for n, (sums, g, top) in enumerate(groups):
        level = level_of(jnp.max(top, axis=1, keepdims=True))
        unit = unit_of(level)
        note = jnp.where(lane == n, level.astype(jnp.int32), note)
        for t in range(tiles):
            out[n * tiles + t] = coded(sums[g * 16 : (g + 1) * 16, t * LANES : (t + 1) * LANES], unit)
    out[len(groups) * tiles] = note.astype(jnp.int16)


SPECS = [
    pl.BlockSpec(memory_space=pltpu.SMEM),
    pl.BlockSpec(memory_space=pl.ANY),
    pl.BlockSpec(memory_space=pl.ANY),
]


VMEM = pl.BlockSpec(memory_space=pltpu.VMEM)


def scratch(part, rows):
    width = part[1]
    return [
        pltpu.VMEM((2, 256, 256), jnp.bfloat16),
        pltpu.VMEM((2, 256, width), jnp.bfloat16),
        pltpu.VMEM((2, rows, width), jnp.float32),
        pltpu.SemaphoreType.DMA((5,)),
    ]


def codes_of(groups, part):
    return jax.ShapeDtypeStruct((groups * part[1] // LANES + 1, 16, LANES), jnp.int16)


def sums_of(rows, part):
    return jax.ShapeDtypeStruct((2, rows, part[1]), jnp.float32)


COST = pl.CostEstimate(flops=4 * 64 * 256 * 4096, bytes_accessed=6 << 20, transcendentals=0)


def call(kernel, outs, work, ins, params=PARAMS, inputs=3):
    return pl.pallas_call(
        kernel,
        in_specs=SPECS[:inputs] + [VMEM] * (len(ins) - inputs),
        out_shape=outs,
        scratch_shapes=work,
        compiler_params=params,
        cost_estimate=COST,
    )(*ins)


def codes_for(steps, *ins):
    return call(functools.partial(codes_kernel, steps), [codes_of(4, PART_A)] * 2, scratch(PART_A, 64), ins)


def own_kernel(me_ref, acts_ref, grads_ref, a0, b0, a1, b1, out0, out1, kept, *work):
    received = [[(a0, 0), (b0, 0)], [(a1, 0), (b1, 0)]]
    tops = add_up(PART_A, rows_a((0, 0)), me_ref, acts_ref, grads_ref, received, *work)
    sums = work[2]
    for e, out in enumerate((out0, out1)):
        write_groups(out, [(sums.at[e], g, tops[e][g]) for g in range(2)])
        kept[e] = sums[e, 32:]


def own_codes(*ins):
    return call(own_kernel, [codes_of(2, PART_A)] * 2 + [sums_of(32, PART_A)], scratch(PART_A, 64), ins)


def pair_kernel(kept, got0, got1, out, rest, sums):
    tiles = PART_A[1] // LANES
    tops = []
    for e, got in enumerate((got0, got1)):
        note = decoded(got[2 * tiles])
        for g in range(2):
            scale = step_of(note[:, g : g + 1])
            top = jnp.zeros((16, LANES), jnp.float32)
            for t in range(tiles):
                cols = slice(t * LANES, (t + 1) * LANES)
                total = kept[e, g * 16 : (g + 1) * 16, cols] + decoded(got[g * tiles + t]) * scale
                if g == 0:
                    sums[e, :, cols] = total
                    top = jnp.maximum(top, jnp.abs(total))
                else:
                    rest[e, :, cols] = total
            if g == 0:
                tops.append(top)
    write_groups(out, [(sums.at[e], 0, tops[e]) for e in range(2)])


def pair_codes(*ins):
    outs = [codes_of(2, PART_A), sums_of(16, PART_A)]
    return call(pair_kernel, outs, [pltpu.VMEM((2, 16, PART_A[1]), jnp.float32)], ins, inputs=0)


def across_first_kernel(me_ref, acts_ref, grads_ref, out, *work):
    tops = add_up(PART_B, rows_b(0, 0), me_ref, acts_ref, grads_ref, [[], []], *work)
    write_groups(out, [(work[2].at[e], g, tops[e][g]) for e in range(2) for g in range(8)])


def across_first(*ins):
    return call(across_first_kernel, codes_of(16, PART_B), scratch(PART_B, 128), ins, FIRST_PARAMS)


def near_kernel(me_ref, acts_ref, grads_ref, got, out0, out1, *work):
    received = [[(got, e * 8)] for e in range(2)]
    tops = add_up(PART_B, rows_b(0, 1, 0), me_ref, acts_ref, grads_ref, received, *work)
    for e, out in enumerate((out0, out1)):
        write_groups(out, [(work[2].at[e], g, tops[e][g]) for g in range(4)])


def near_codes(*ins):
    return call(near_kernel, [codes_of(4, PART_B)] * 2, scratch(PART_B, 64), ins)


def along_x_kernel(me_ref, acts_ref, grads_ref, got, near0, near1, out1, out2, out3, *work):
    received = [[(got, e * 8 + 5), ((near0, near1)[e], 1)] for e in range(2)]
    tops = add_up(PART_B, rows_b(1, 1, 1), me_ref, acts_ref, grads_ref, received, *work)
    for k, out in enumerate((out1, out2, out3)):
        write_groups(out, [(work[2].at[e], k, tops[e][k]) for e in range(2)])


def along_x(*ins):
    return call(along_x_kernel, [codes_of(2, PART_B)] * 3, scratch(PART_B, 48), ins)


def own_b_kernel(me_ref, acts_ref, grads_ref, got, near0, near1, r1, r2, r3, out, *work):
    received = [[(got, e * 8 + 4), ((near0, near1)[e], 0)] + [(r, e) for r in (r1, r2, r3)] for e in range(2)]
    add_up(PART_B, rows_b(0, 1, 1), me_ref, acts_ref, grads_ref, received, *work)
    out[...] = work[2][...]


def own_b(*ins):
    return call(own_b_kernel, sums_of(16, PART_B), scratch(PART_B, 16), ins)


def join_kernel(rest, got, own, *refs):
    *outs, sums = refs
    tiles = PART_A[1] // LANES
    note = decoded(got[2 * tiles])
    for e in range(2):
        scale = step_of(note[:, e : e + 1])
        for t in range(tiles):
            cols = slice(t * LANES, (t + 1) * LANES)
            sums[e, :, cols] = rest[e, :, cols] + decoded(got[e * tiles + t]) * scale
        sums[e, :, PART_B[0] :] = own[e]
    upper = lax.broadcasted_iota(jnp.int32, (8, 1), 0) < 4
    for pair in range(2):
        tile = slice(pair * 8, pair * 8 + 8)
        z = [[sums[e, tile, h * BLOCK : (h + 1) * BLOCK] for h in range(2)] for e in range(2)]
        even = [jnp.where(upper, z[0][h], pltpu.roll(z[1][h], 4, 0)) for h in range(2)]
        odd = [jnp.where(upper, pltpu.roll(z[0][h], 4, 0), z[1][h]) for h in range(2)]
        for out, halves in ((outs[pair * 2], even), (outs[pair * 2 + 1], odd)):
            values = jnp.concatenate(halves, axis=0)
            top = lane_max(jnp.zeros((16, LANES), jnp.float32), values)
            level = level_of(jnp.max(top, axis=1, keepdims=True))
            unit = unit_of(level)
            for t in range(16):
                out[t] = coded(values[:, t * LANES : (t + 1) * LANES], unit)
            out[16] = to_short(jnp.broadcast_to(level, (16, LANES)))


def join(*ins):
    outs = [jax.ShapeDtypeStruct((17, 16, LANES), jnp.int16)] * 4
    return call(join_kernel, outs, [pltpu.VMEM((2, 16, 2 * BLOCK), jnp.float32)], ins, inputs=0)


def adam_kernel(c0, c1, c2, c3, master, m_codes, m_scale, v_codes, v_scale,
                new_master, m_state, m_absmax, v_state, v_absmax, rollout, grad):
    codes = (c0, c1, c2, c3)
    tiles = BLOCK // LANES
    steps = [step_of(decoded(c[tiles])[:, :1]) for c in codes]
    for t in range(tiles):
        total = decoded(c0[t]) * steps[0]
        for s in range(1, 4):
            total = total + decoded(codes[s][t]) * steps[s]
        for h in range(2):
            grad[:, (h * tiles + t) * LANES : (h * tiles + t + 1) * LANES] = total[h * 8 : (h + 1) * 8]
    diagonal = lax.broadcasted_iota(jnp.int32, (4, 4), 0) == lax.broadcasted_iota(jnp.int32, (4, 4), 1)

    def upright(row):
        return jnp.sum(jnp.where(diagonal, row, 0.0), axis=1, keepdims=True)

    def level_row(column):
        return jnp.sum(jnp.where(diagonal, column, 0.0), axis=0, keepdims=True)

    for e in range(2):
        for b in range(2):
            cols = slice(b * BLOCK, (b + 1) * BLOCK)
            g = grad[e * 4 : (e + 1) * 4, cols]
            m_old = m_codes[e, :, cols].astype(jnp.float32) * (upright(m_scale[e, b : b + 1, :]) / 127.0)
            v_old = v_codes[e, :, cols].astype(jnp.float32) * (upright(v_scale[e, b : b + 1, :]) / 255.0)
            m_new = beta_first * m_old + (1.0 - beta_first) * g
            v_new = beta_second * v_old + (1.0 - beta_second) * g * g
            update = m_new / first_bias / (jnp.sqrt(v_new / second_bias) + adam_eps)
            old = master[e, :, cols]
            new = old - learn_rate * (update + decay_rate * old)
            new_master[e, :, cols] = new
            m_top = jnp.max(jnp.abs(m_new), axis=1, keepdims=True)
            v_top = jnp.max(v_new, axis=1, keepdims=True)
            m_absmax[e, b : b + 1, :] = level_row(m_top)
            v_absmax[e, b : b + 1, :] = level_row(v_top)
            m_state[e, :, cols] = m_new / (m_top + scale_eps)
            v_state[e, :, cols] = v_new / (v_top + scale_eps)
            grad[e * 4 : (e + 1) * 4, cols] = new
    for k in range(16):
        for h in range(2):
            at = k * 256 + h * LANES
            tile = grad[:, at : at + LANES].astype(jnp.bfloat16)
            for copy in range(2):
                rollout[copy * 16 + k, h * 8 : (h + 1) * 8, :] = tile


def adam(codes, master, m_codes, m_scale, v_codes, v_scale):
    big = jax.ShapeDtypeStruct((2, 4, 4096), jnp.float32)
    small = jax.ShapeDtypeStruct((2, 2, 4), jnp.float32)
    new_master, m_state, m_absmax, v_state, v_absmax, weights = pl.pallas_call(
        adam_kernel,
        out_shape=[big, big, small, big, small, jax.ShapeDtypeStruct((32, 16, LANES), jnp.bfloat16)],
        scratch_shapes=[pltpu.VMEM((8, 4096), jnp.float32)],
        compiler_params=PARAMS,
        cost_estimate=pl.CostEstimate(flops=2 * 4 * 4096 * 40, bytes_accessed=2 << 20, transcendentals=0),
    )(*codes, master, m_codes, jnp.swapaxes(m_scale, 1, 2), v_codes, jnp.swapaxes(v_scale, 1, 2))
    return new_master, m_state, jnp.swapaxes(m_absmax, 1, 2), v_state, jnp.swapaxes(v_absmax, 1, 2), weights


def push_weights(weights):
    plane, group = lax.axis_index("dp") // 16, lax.axis_index("group")
    swapped = lax.all_to_all(
        weights, ("dp", "group"), 0, 0, axis_index_groups=swap_groups(), tiled=True
    )
    upper = jnp.where(plane == group, plane % 2 == 1, plane > group)
    slab = jnp.where(upper, swapped[16:], swapped[:16])
    slab = jnp.transpose(slab.reshape(16, 2, 2, 4, LANES), (2, 0, 3, 1, 4)).reshape(2, 64, 256)
    return lax.all_gather(slab, "group", axis=1, tiled=True)


def on_device(acts, out_grads, master, m_codes, m_scale, v_codes, v_scale):
    me = lax.axis_index("dp").reshape(1).astype(jnp.int32)

    inputs = (me, acts, out_grads)

    def send(codes, pairs):
        return lax.ppermute(codes, "dp", pairs)

    far0, far1 = codes_for((2, 2), *inputs)
    far0, far1 = send(far0, UP), send(far1, DOWN)
    crossed = send(across_first(*inputs), ACROSS)
    down0, up1 = codes_for((3, 1), *inputs)
    down0, up1 = send(down0, DOWN), send(up1, UP)
    up0, down1 = codes_for((1, 3), *inputs, far0, far1)
    up0, down1 = send(up0, UP), send(down1, DOWN)
    there0, there1 = near_codes(*inputs, crossed)
    acts, _ = lax.optimization_barrier((acts, there0))
    there0, there1 = send(there0, PAIR[0]), send(there1, PAIR[1])
    inputs = (me, acts, out_grads)
    near0, near1, kept = own_codes(*inputs, down0, up0, up1, down1)
    near0, near1 = send(near0, PAIR[0]), send(near1, PAIR[1])
    steps = along_x(*inputs, crossed, there0, there1)
    kept, _ = lax.optimization_barrier((kept, steps[0]))
    two = send(steps[1], TWO)
    steps = [send(steps[0], UP), two, send(steps[2], DOWN)]
    across, rest = pair_codes(kept, near0, near1)
    across = send(across, ACROSS)
    own = own_b(*inputs, crossed, there0, there1, *steps)
    codes = join(rest, across, own)
    far = send(codes[2], z_shift(2))
    codes = [codes[0], send(codes[1], z_shift(1)), far, send(codes[3], z_shift(3))]
    *state, weights = adam(codes, master, m_codes, m_scale, v_codes, v_scale)
    return (*state, push_weights(weights))


def solution(mesh):
    split = P(None, "dp", "group")
    return jax.shard_map(
        on_device,
        mesh=mesh,
        in_specs=(P(None, "dp", None),) + (split,) * 6,
        out_specs=(split,) * 5 + (P(None, None, "dp"),),
        check_vma=False,
    )
```
